128 devices in a mesh: dp: 2 (over z_hi), seq: 32 (over y, x, z_lo), tp: 2 (over core).
Axes of the slice: x: 4, y: 4, z: 4 (z_hi: 2, z_lo: 2; z = z_hi * 2 + z_lo), core: 2. Of those that a mesh axis runs over, the one named last changes fastest.
Arguments:
- bases: int32 [2, 49152], P('dp', 'seq'), may hold values from -2147483648 to 2147483646
- shifts: int32 [2], P('dp'), may hold values from -6144 to 6144
- embed_weight: bfloat16 [512, 768], replicated, may hold values from -0.5 to 0.5
- conv_weight: bfloat16 [5, 768, 1536], P(None, None, 'tp'), may hold values from -0.09375 to 0.09375
- query_weight: bfloat16 [1536, 1536], P(None, 'tp'), may hold values from -0.15625 to 0.15625
- keyvalue_weight: bfloat16 [1536, 2, 256], P(None, 'tp'), may hold values from -0.15625 to 0.15625
- output_weight: bfloat16 [1536, 1536], P('tp'), may hold values from -0.15625 to 0.15625
- slopes: float32 [12], P('tp'), may hold values from 0.1 to 16
- cotangent: bfloat16 [2, 6144, 1536], P('dp', 'seq', 'tp'), may hold values from -6 to 6
Outputs:
- result: bfloat16 [2, 6144, 1536], P('dp', 'seq', 'tp')
- grad_embed: float32 [512, 768], P('seq')
- grad_conv: float32 [5, 768, 1536], P(None, 'seq', 'tp')
- grad_query: float32 [1536, 1536], P('seq', 'tp')
- grad_keyvalue: float32 [1536, 2, 256], P('seq', 'tp')
- grad_output: float32 [1536, 1536], P('tp', 'seq')
The draws below stay inside these ranges and needn't reach their ends.
Inputs may be any that keep to these rules, and one draw needn't show every extreme that they name: Word w of a sample holds the sample's bases 16 w to 16 w + 15; base 16 w + r is the two-bit field at bits 2 r and 2 r + 1 of the word's two's-complement pattern, 0 to 3 standing for A, C, G, T.
All inputs are finite; a program needn't handle non-finite values.
Results may differ from the reference program's by a relative error of at most 0.039.
Values may be sent and summed in bfloat16 or wider, within the bound.
A program may use at most 128 MiB of HBM per device.

```python
import math
import jax
import jax.numpy as jnp
from jax import lax

CONV_IN = 768
WIDTH = 1536
TAPS = 5
BASES_TOK = 128
HEADS = 12
HEAD_DIM = 128
KV_HEADS = 2
SEQ_LEN = 6144
SAMPLES = 2
ROWS = 12288


def plant(drawn, stream_key, smallest, largest):
    dims = drawn.shape
    index_at = [jax.random.randint(jax.random.fold_in(stream_key, axis), (), 0, dims[axis]) for axis in range(len(dims))]
    drawn = drawn.at[tuple(index_at)].set(smallest)
    longest = dims.index(max(dims))
    index_at[longest] = (index_at[longest] + 1) % dims[longest]
    return drawn.at[tuple(index_at)].set(largest)


def block_scale(own_key, dims, split, low, top_value):
    gain = 1.0
    for position, blocks in split:
        steps = jax.random.uniform(jax.random.fold_in(jax.random.fold_in(own_key, 6), position), (blocks,), jnp.float32, low / len(split), top_value / len(split))
        gain = gain * jnp.repeat(jnp.exp(steps), dims[position] // blocks).reshape((-1,) + (1,) * (len(dims) - 1 - position))
    return gain


def centred(own_key, dims, spread, reach, cuts=(), kind=jnp.bfloat16):
    values = spread * jax.random.normal(own_key, dims, jnp.float32)
    if cuts:
        values = values * block_scale(own_key, dims, cuts, -0.22, 0.18)
    return jnp.clip(values, -reach, reach).astype(kind)


def setup_inputs(seed: int = 0) -> dict:
    streams_of = jax.random.split(jax.random.key(seed), 10)
    bases = plant(jax.random.randint(streams_of[0], (SAMPLES, SEQ_LEN * BASES_TOK // 16), -2147483648, 2147483647), jax.random.fold_in(streams_of[0], 1), -2147483648, 2147483646).astype(jnp.int32)
    shifts = jax.random.randint(streams_of[1], (SAMPLES,), 0 - SEQ_LEN, SEQ_LEN + 1).astype(jnp.int32)
    embed_weight = centred(streams_of[2], (4 * BASES_TOK, CONV_IN), BASES_TOK ** -0.5, 0.5)
    conv_weight = centred(streams_of[3], (TAPS, CONV_IN, WIDTH), (TAPS * CONV_IN) ** -0.5, 0.09375, ((2, 2),))
    query_weight = centred(streams_of[4], (WIDTH, HEADS * HEAD_DIM), WIDTH ** -0.5, 0.15625, ((1, 2),))
    keyvalue_weight = centred(streams_of[5], (WIDTH, KV_HEADS, 2 * HEAD_DIM), WIDTH ** -0.5, 0.15625, ((1, 2),))
    output_weight = centred(streams_of[6], (HEADS * HEAD_DIM, WIDTH), (HEADS * HEAD_DIM) ** -0.5, 0.15625, ((0, 2),))
    slopes = jnp.clip(jnp.exp(math.log(16.0) - 5.075174 * jax.random.uniform(streams_of[7], (HEADS,), jnp.float32) ** block_scale(streams_of[7], (HEADS,), ((0, 2),), -0.2, 0.2)), 0.1, 16.0)
    cotangent = centred(streams_of[8], (SAMPLES, SEQ_LEN, WIDTH), 1.0, 6.0, ((0, 2), (1, 32), (2, 2)))
    return {"bases": bases, "shifts": shifts, "embed_weight": embed_weight, "conv_weight": conv_weight, "query_weight": query_weight, "keyvalue_weight": keyvalue_weight, "output_weight": output_weight, "slopes": slopes, "cotangent": cotangent}


ROOT_TWO_PI = math.sqrt(2.0 / math.pi)
CUBIC = 0.044715
EPSILON = 1e-06
DISTANCE_SCALE = 128.0

def gelu_value(inputs):
    return 0.5 * inputs * (1.0 + jnp.tanh(ROOT_TWO_PI * (inputs + CUBIC * inputs * inputs * inputs)))

def gelu_slope(inputs):
    inner = jnp.tanh(ROOT_TWO_PI * (inputs + CUBIC * inputs * inputs * inputs))
    return 0.5 * (1.0 + inner) + 0.5 * inputs * (1.0 - inner * inner) * ROOT_TWO_PI * (1.0 + 3.0 * CUBIC * inputs * inputs)

def inverse_rms(values):
    return lax.rsqrt(lax.optimization_barrier(jnp.mean(values * values, axis=-1, keepdims=True)) + EPSILON)

def unpack_bases(packed):
    leading = packed.shape[:-1]
    shift_bits = 2 * jnp.arange(16, dtype=jnp.int32)
    fields = jnp.right_shift(packed[..., None], shift_bits) & 3
    letters = fields.reshape(leading + (-1, BASES_TOK))
    onehot = letters[..., None] == jnp.arange(4, dtype=jnp.int32)
    return onehot.reshape(leading + (letters.shape[-2], 4 * BASES_TOK)).astype(jnp.bfloat16)

def position_bias(slope_table, query_pos, key_pos, offset):
    distance = jnp.abs(query_pos[:, None] - key_pos[None, :] + offset).astype(jnp.float32)
    return -(slope_table[None, :, :, None] * distance[:, None, None, :]) / DISTANCE_SCALE

def block_rows_of():
    if SEQ_LEN > 512 and SEQ_LEN % 512 == 0:
        return 512
    return SEQ_LEN

def attend_sample(query, keyvalue, slope_table, offset):
    members = HEADS // KV_HEADS
    block_rows = block_rows_of()
    keys_all = keyvalue[:, :, :HEAD_DIM].astype(jnp.float32)
    values_all = keyvalue[:, :, HEAD_DIM:].astype(jnp.float32)
    key_pos = jnp.arange(SEQ_LEN, dtype=jnp.int32)
    grouped = query.reshape(SEQ_LEN, KV_HEADS, members, HEAD_DIM)

    def one_block(first_row):
        rows_now = lax.dynamic_slice_in_dim(grouped, first_row, block_rows, 0).astype(jnp.float32)
        query_pos = first_row + jnp.arange(block_rows, dtype=jnp.int32)
        scores = jnp.einsum('qgmd,kgd->qgmk', rows_now, keys_all) / math.sqrt(HEAD_DIM)
        scores = scores + position_bias(slope_table, query_pos, key_pos, offset)
        highest = lax.optimization_barrier(jnp.max(scores, axis=-1))
        weights = jnp.exp(scores - highest[..., None])
        totals = lax.optimization_barrier(jnp.sum(weights, axis=-1))
        rounded = lax.optimization_barrier(weights.astype(jnp.bfloat16)).astype(jnp.float32)
        mixed_rows = jnp.einsum('qgmk,kgd->qgmd', rounded, values_all) / totals[..., None]
        return (mixed_rows.astype(jnp.bfloat16).reshape(block_rows, HEADS * HEAD_DIM), highest + jnp.log(totals))
    starts = jnp.arange(0, SEQ_LEN, block_rows, dtype=jnp.int32)
    outputs, log_totals = lax.map(one_block, starts)
    return (outputs.reshape(SEQ_LEN, HEADS * HEAD_DIM), log_totals.reshape(SEQ_LEN, KV_HEADS, members))

def attend_back(query, keyvalue, attended, log_totals, back_attended, slope_table, offset):
    members = HEADS // KV_HEADS
    block_rows = block_rows_of()
    keys_all = keyvalue[:, :, :HEAD_DIM].astype(jnp.float32)
    values_all = keyvalue[:, :, HEAD_DIM:].astype(jnp.float32)
    key_pos = jnp.arange(SEQ_LEN, dtype=jnp.int32)
    grouped = query.reshape(SEQ_LEN, KV_HEADS, members, HEAD_DIM)
    back_grouped = back_attended.reshape(SEQ_LEN, KV_HEADS, members, HEAD_DIM)
    attended_grouped = attended.reshape(SEQ_LEN, KV_HEADS, members, HEAD_DIM)
    deltas = lax.optimization_barrier(jnp.sum(back_grouped.astype(jnp.float32) * attended_grouped.astype(jnp.float32), axis=-1))

    def one_block(running, first_row):
        rows_now = lax.dynamic_slice_in_dim(grouped, first_row, block_rows, 0).astype(jnp.float32)
        back_now = lax.dynamic_slice_in_dim(back_grouped, first_row, block_rows, 0).astype(jnp.float32)
        delta_now = lax.dynamic_slice_in_dim(deltas, first_row, block_rows, 0)
        totals_now = lax.dynamic_slice_in_dim(log_totals, first_row, block_rows, 0)
        query_pos = first_row + jnp.arange(block_rows, dtype=jnp.int32)
        scores = jnp.einsum('qgmd,kgd->qgmk', rows_now, keys_all) / math.sqrt(HEAD_DIM)
        scores = scores + position_bias(slope_table, query_pos, key_pos, offset)
        probs = jnp.exp(scores - totals_now[..., None])
        probs_low = lax.optimization_barrier(probs.astype(jnp.bfloat16)).astype(jnp.float32)
        value_grad = jnp.einsum('qgmk,qgmd->kgd', probs_low, back_now)
        back_probs = jnp.einsum('qgmd,kgd->qgmk', back_now, values_all)
        grad_scores = (probs * (back_probs - delta_now[..., None]) / math.sqrt(HEAD_DIM)).astype(jnp.bfloat16)
        grad_scores = lax.optimization_barrier(grad_scores).astype(jnp.float32)
        query_grad = jnp.einsum('qgmk,kgd->qgmd', grad_scores, keys_all).astype(jnp.bfloat16)
        key_grad = jnp.einsum('qgmk,qgmd->kgd', grad_scores, rows_now)
        running = running + jnp.concatenate([key_grad, value_grad], axis=-1)
        return (running, query_grad.reshape(block_rows, HEADS * HEAD_DIM))
    starts = jnp.arange(0, SEQ_LEN, block_rows, dtype=jnp.int32)
    running_start = jnp.zeros((SEQ_LEN, KV_HEADS, 2 * HEAD_DIM), jnp.float32)
    pair_total, query_grads = lax.scan(one_block, running_start, starts)
    return (query_grads.reshape(SEQ_LEN, HEADS * HEAD_DIM), pair_total.astype(jnp.bfloat16))

def reference(bases, shifts, embed_weight, conv_weight, query_weight, keyvalue_weight, output_weight, slopes, cotangent):
    patches = unpack_bases(bases)
    flat_patches = patches.reshape(-1, 4 * BASES_TOK)
    embedded = jnp.dot(flat_patches, embed_weight, preferred_element_type=jnp.float32).astype(jnp.bfloat16)
    embedded_wide = embedded.astype(jnp.float32).reshape(SAMPLES, SEQ_LEN, CONV_IN)
    scale_in = inverse_rms(embedded_wide)
    normed_in = embedded_wide * scale_in
    activated = gelu_value(normed_in).astype(jnp.bfloat16)
    reach_rows = TAPS // 2
    padded = jnp.pad(activated, ((0, 0), (reach_rows, reach_rows), (0, 0)))
    windows = jnp.concatenate([padded[:, tap_index:tap_index + SEQ_LEN] for tap_index in range(TAPS)], axis=-1)
    windows = windows.reshape(-1, TAPS * CONV_IN)
    convolved = jnp.dot(windows, conv_weight.reshape(TAPS * CONV_IN, WIDTH), preferred_element_type=jnp.float32)
    convolved = convolved.reshape(SAMPLES, SEQ_LEN, WIDTH)
    hidden = (convolved + jnp.tile(embedded_wide, (1, 1, WIDTH // CONV_IN))).astype(jnp.bfloat16)
    hidden_wide = hidden.astype(jnp.float32)
    scale_mid = inverse_rms(hidden_wide)
    normed_wide = hidden_wide * scale_mid
    normed = normed_wide.astype(jnp.bfloat16).reshape(-1, WIDTH)
    queries = jnp.dot(normed, query_weight, preferred_element_type=jnp.float32).astype(jnp.bfloat16)
    queries = queries.reshape(SAMPLES, SEQ_LEN, HEADS * HEAD_DIM)
    pair_weight = keyvalue_weight.reshape(WIDTH, KV_HEADS * 2 * HEAD_DIM)
    keyvalues = jnp.dot(normed, pair_weight, preferred_element_type=jnp.float32).astype(jnp.bfloat16)
    keyvalues = keyvalues.reshape(SAMPLES, SEQ_LEN, KV_HEADS, 2 * HEAD_DIM)
    slope_table = slopes.reshape(KV_HEADS, HEADS // KV_HEADS)
    attended_list = []
    totals_list = []
    for sample_index in range(SAMPLES):
        attended_one, totals_one = attend_sample(queries[sample_index], keyvalues[sample_index], slope_table, shifts[sample_index])
        attended_list.append(attended_one)
        totals_list.append(totals_one)
    attended = jnp.stack(attended_list)
    attended_flat = attended.reshape(-1, HEADS * HEAD_DIM)
    projected = jnp.dot(attended_flat, output_weight, preferred_element_type=jnp.float32).reshape(SAMPLES, SEQ_LEN, WIDTH)
    result = (hidden_wide + projected).astype(jnp.bfloat16)
    cotangent_flat = cotangent.reshape(-1, WIDTH)
    back_attended = jnp.dot(cotangent_flat, output_weight.T, preferred_element_type=jnp.float32).astype(jnp.bfloat16)
    back_attended = back_attended.reshape(SAMPLES, SEQ_LEN, HEADS * HEAD_DIM)
    grad_output = jnp.dot(attended_flat.T, cotangent_flat, preferred_element_type=jnp.float32)
    query_list = []
    pair_list = []
    for sample_index in range(SAMPLES):
        query_back, pair_back = attend_back(queries[sample_index], keyvalues[sample_index], attended[sample_index], totals_list[sample_index], back_attended[sample_index], slope_table, shifts[sample_index])
        query_list.append(query_back)
        pair_list.append(pair_back)
    back_query = jnp.stack(query_list).reshape(-1, HEADS * HEAD_DIM)
    back_pair = jnp.stack(pair_list).reshape(-1, KV_HEADS * 2 * HEAD_DIM)
    grad_query = jnp.dot(normed.T, back_query, preferred_element_type=jnp.float32)
    grad_pair = jnp.dot(normed.T, back_pair, preferred_element_type=jnp.float32).reshape(WIDTH, KV_HEADS, 2 * HEAD_DIM)
    back_normed = jnp.dot(back_query, query_weight.T, preferred_element_type=jnp.float32)
    back_normed = back_normed + jnp.dot(back_pair, pair_weight.T, preferred_element_type=jnp.float32)
    back_normed = back_normed.reshape(SAMPLES, SEQ_LEN, WIDTH)
    back_hidden = cotangent.astype(jnp.float32) + scale_mid * (back_normed - normed_wide * lax.optimization_barrier(jnp.mean(back_normed * normed_wide, axis=-1, keepdims=True)))
    back_conv = back_hidden.astype(jnp.bfloat16)
    grad_conv = jnp.dot(windows.T, back_conv.reshape(-1, WIDTH), preferred_element_type=jnp.float32).reshape(TAPS, CONV_IN, WIDTH)
    back_padded = jnp.pad(back_conv, ((0, 0), (reach_rows, reach_rows), (0, 0)))
    back_windows = jnp.concatenate([back_padded[:, TAPS - 1 - tap_index:TAPS - 1 - tap_index + SEQ_LEN] for tap_index in range(TAPS)], axis=-1)
    back_windows = back_windows.reshape(-1, TAPS * WIDTH)
    turned = jnp.transpose(conv_weight, (0, 2, 1)).reshape(TAPS * WIDTH, CONV_IN)
    back_active = jnp.dot(back_windows, turned, preferred_element_type=jnp.float32).reshape(SAMPLES, SEQ_LEN, CONV_IN)
    back_normed_in = back_active * gelu_slope(normed_in)
    back_residual = lax.optimization_barrier(jnp.sum(back_hidden.reshape(SAMPLES, SEQ_LEN, WIDTH // CONV_IN, CONV_IN), axis=2))
    back_embedded = back_residual + scale_in * (back_normed_in - normed_in * lax.optimization_barrier(jnp.mean(back_normed_in * normed_in, axis=-1, keepdims=True)))
    back_embedded = back_embedded.astype(jnp.bfloat16).reshape(-1, CONV_IN)
    grad_embed = jnp.dot(flat_patches.T, back_embedded, preferred_element_type=jnp.float32)
    factor = ROWS ** (-0.5)
    return (result, grad_embed * factor, grad_conv * factor, grad_query * factor, grad_pair * factor, grad_output * factor)
```

```python
import functools
import math

import jax
import jax.numpy as jnp
import numpy as np
from jax import lax
from jax.experimental import pallas as pl
from jax.experimental.pallas import tpu as pltpu
from jax.sharding import PartitionSpec as P

ROOT_TWO_PI = math.sqrt(2.0 / math.pi)
CUBIC = 0.044715
EPSILON = 1e-06
DISTANCE_SCALE = 128.0
MESH = pl.DeviceIdType.MESH
LOG2E = math.log2(math.e)
VMEM_LIMIT = 60 * 1024 * 1024

TOK = 192
HEAD = 128
MEMBERS = 6
QW = MEMBERS * HEAD
SCORE_SCALE = LOG2E / math.sqrt(HEAD)
BIAS_SCALE = LOG2E / DISTANCE_SCALE

KV_PARTS = 4
KV_ROWS = TOK // KV_PARTS


def flip(value, low, high):
    value = value + low * (1 - 2 * (value % 2))
    return value + high * (3 - 2 * value)


def seq_peer(seq, moves):
    y, x, z = seq // 8, (seq // 2) % 4, seq % 2
    y = flip(y, moves[2], moves[3])
    x = flip(x, moves[0], moves[1])
    z = z + moves[4] * (1 - 2 * z)
    return (y * 4 + x) * 2 + z


def one_move(seq, direction):
    return seq_peer(seq, [1 if d == direction else 0 for d in range(5)])


def kv_mask(part, place, z):
    bits = [(place >> ((d - part) % 4)) & 1 for d in range(4)]
    x = bits[0] ^ (3 * bits[1])
    y = bits[2] ^ (3 * bits[3])
    return (y << 3) | (x << 1) | z


KV_MASKS = np.array(
    [[[kv_mask(q, p, z) for z in range(2)] for q in range(KV_PARTS)] for p in range(16)], np.int32
)


def enter(peers):
    barrier = pltpu.get_barrier_semaphore()
    for peer in peers:
        pl.semaphore_signal(barrier, inc=1, device_id=peer, device_id_type=MESH)
    pl.semaphore_wait(barrier, len(peers))


def send(src, dst, send_sem, recv_sem, peer):
    return pltpu.make_async_remote_copy(
        src_ref=src,
        dst_ref=dst,
        send_sem=send_sem,
        recv_sem=recv_sem,
        device_id=peer,
        device_id_type=MESH,
    )


NT = (((1,), (1,)), ((), ()))
TN = (((0,), (0,)), ((), ()))


def dot_nt(a, b):
    return lax.dot_general(a, b, NT, preferred_element_type=jnp.float32)


def dot_tn(a, b):
    return lax.dot_general(a, b, TN, preferred_element_type=jnp.float32)


def dot_nn(a, b):
    return jnp.dot(a, b, preferred_element_type=jnp.float32)


def forward_kernel(
    slope_ref, q_ref, kv_ref, back_ref, qpos_ref, kpos_ref,
    att_ref, stat_ref, held_ref,
    acc_ref, top_ref, send_sem, recv_sem, zsend_sem, zrecv_sem,
):
    seq = lax.axis_index("seq")
    peers = [{"seq": one_move(seq, d)} for d in range(5)]
    enter(peers)
    zcopies = []
    for part in range(KV_PARTS):
        rows = pl.ds(part * KV_ROWS, KV_ROWS)
        copy = send(
            kv_ref.at[rows],
            held_ref.at[0, part, pl.ds(KV_ROWS, KV_ROWS)],
            zsend_sem.at[part],
            zrecv_sem.at[part],
            peers[4],
        )
        copy.start()
        zcopies.append(copy)
    for part in range(KV_PARTS):
        held_ref[0, part, 0:KV_ROWS] = kv_ref[part * KV_ROWS : (part + 1) * KV_ROWS]
    acc_ref[...] = jnp.zeros_like(acc_ref)
    top_ref[...] = jnp.full_like(top_ref, -1e30)
    qpos = qpos_ref[...]

    def absorb(pair, kpos):
        keys = pair[:, :HEAD]
        values = jnp.concatenate([pair[:, HEAD:], jnp.ones_like(keys)], axis=1)
        distance = jnp.abs(qpos - kpos)
        for head in range(MEMBERS):
            scores = dot_nt(q_ref[:, head * HEAD : (head + 1) * HEAD], keys) * SCORE_SCALE
            scores = scores - distance * (slope_ref[head] * BIAS_SCALE)
            old = top_ref[head]
            new = jnp.maximum(old, jnp.max(scores, axis=1, keepdims=True))
            fading = jnp.exp2(old - new)
            weights = jnp.exp2(scores - new[:, :1]).astype(jnp.bfloat16)
            acc_ref[head] = acc_ref[head] * jnp.concatenate([fading, fading], axis=1) + dot_nn(
                weights, values
            )
            top_ref[head] = new

    def places(first, count):
        pair = held_ref[pl.ds(first, count)].reshape(count * 2 * TOK, 2 * HEAD)
        if count == 1:
            kpos = kpos_ref[first]
        else:
            kpos = jnp.concatenate([kpos_ref[first + i] for i in range(count)], axis=1)
        absorb(pair, kpos)

    def start_stage(k):
        copies = []
        for part in range(KV_PARTS):
            copy = send(
                held_ref.at[pl.ds(0, 2**k), part],
                held_ref.at[pl.ds(2**k, 2**k), part],
                send_sem.at[k, part],
                recv_sem.at[k, part],
                peers[(part + k) % 4],
            )
            copy.start()
            copies.append(copy)
        return copies

    for copy in zcopies:
        copy.wait()
    stage = start_stage(0)
    places(0, 1)
    for copy in stage:
        copy.wait()
    stage = start_stage(1)
    places(1, 1)
    for copy in stage:
        copy.wait()
    stage = start_stage(2)
    places(2, 2)
    for copy in stage:
        copy.wait()
    stage = start_stage(3)

    def two_places(first):
        def step(i, carry):
            places(first + 2 * i, 2)
            return carry

        return step

    lax.fori_loop(0, 2, two_places(4), 0)
    for copy in stage:
        copy.wait()
    lax.fori_loop(0, 4, two_places(8), 0)
    lane = lax.broadcasted_iota(jnp.int32, (TOK, HEAD), 1)
    stats = jnp.zeros((TOK, HEAD), jnp.float32)
    for head in range(MEMBERS):
        totals = acc_ref[head, :, HEAD:]
        mixed = (acc_ref[head, :, :HEAD] / totals).astype(jnp.bfloat16)
        att_ref[:, head * HEAD : (head + 1) * HEAD] = mixed
        back = back_ref[:, head * HEAD : (head + 1) * HEAD].astype(jnp.float32)
        delta = jnp.sum(back * mixed.astype(jnp.float32), axis=1, keepdims=True)
        stats = jnp.where(lane == head, top_ref[head] + jnp.log2(totals), stats)
        stats = jnp.where(lane == 8 + head, delta, stats)
    stat_ref[...] = stats


def forward_attention(slopes, queries, keyvalue, back_attended, qpos, kpos):
    vmem = pl.BlockSpec(memory_space=pltpu.VMEM)
    return pl.pallas_call(
        forward_kernel,
        out_shape=(
            jax.ShapeDtypeStruct((TOK, QW), jnp.bfloat16),
            jax.ShapeDtypeStruct((TOK, HEAD), jnp.float32),
            jax.ShapeDtypeStruct((16, KV_PARTS, 2 * KV_ROWS, 2 * HEAD), jnp.bfloat16),
        ),
        in_specs=[pl.BlockSpec(memory_space=pltpu.SMEM)] + [vmem] * 5,
        out_specs=(vmem, vmem, vmem),
        scratch_shapes=[
            pltpu.VMEM((MEMBERS, TOK, 2 * HEAD), jnp.float32),
            pltpu.VMEM((MEMBERS, TOK, HEAD), jnp.float32),
            pltpu.SemaphoreType.DMA((4, KV_PARTS)),
            pltpu.SemaphoreType.DMA((4, KV_PARTS)),
            pltpu.SemaphoreType.DMA((KV_PARTS,)),
            pltpu.SemaphoreType.DMA((KV_PARTS,)),
        ],
        compiler_params=pltpu.CompilerParams(
            collective_id=0, has_side_effects=True, vmem_limit_bytes=VMEM_LIMIT
        ),
    )(slopes, queries, keyvalue, back_attended, qpos, kpos)


def backward_kernel(
    kbase_ref, q_ref, back_ref, held_ref, qpos_ref, slope_ref, lse_ref, delta_ref,
    dq_ref, dkv_ref,
    qs_ref, bs_ref, dq_acc, part_ref, land3, land2, land1, land0, landz,
    send_sem, recv_sem, zsend_sem, zrecv_sem,
):
    seq = lax.axis_index("seq")
    peers = [{"seq": one_move(seq, d)} for d in range(5)]
    enter(peers)
    lands = [land0, land1, land2, land3]
    for head in range(MEMBERS):
        rows = slice(head * TOK, (head + 1) * TOK)
        qs_ref[rows] = q_ref[:, head * HEAD : (head + 1) * HEAD]
        bs_ref[rows] = back_ref[:, head * HEAD : (head + 1) * HEAD]
    dq_acc[...] = jnp.zeros_like(dq_acc)
    qpos = qpos_ref[...]
    row = lax.broadcasted_iota(jnp.int32, (KV_ROWS, 1), 0).astype(jnp.float32)

    def one_place(place, carry):
        pair = held_ref[place].reshape(2 * TOK, 2 * HEAD)
        keys, values = pair[:, :HEAD], pair[:, HEAD:]
        kpos = jnp.concatenate([row + kbase_ref[place, g] for g in range(8)], axis=0)
        distance = jnp.abs(qpos - kpos)
        key_grad = jnp.zeros((2 * TOK, HEAD), jnp.float32)
        value_grad = jnp.zeros((2 * TOK, HEAD), jnp.float32)
        for duo in range(MEMBERS // 2):
            rows = slice(duo * 2 * TOK, (duo + 1) * 2 * TOK)
            qd, bd = qs_ref[rows], bs_ref[rows]
            scores = dot_nt(keys, qd) * SCORE_SCALE - distance * slope_ref[duo]
            probs = jnp.exp2(scores - lse_ref[duo])
            back_probs = dot_nt(values, bd)
            grad_scores = (probs * (back_probs - delta_ref[duo])).astype(jnp.bfloat16)
            value_grad = value_grad + dot_nn(probs.astype(jnp.bfloat16), bd)
            key_grad = key_grad + dot_nn(grad_scores, qd)
            dq_acc[rows] += dot_tn(grad_scores, keys)
        both = jnp.concatenate([key_grad * (1.0 / math.sqrt(HEAD)), value_grad], axis=1)
        part_ref[place] = both.astype(jnp.bfloat16).reshape(KV_PARTS, 2 * KV_ROWS, 2 * HEAD)
        return carry

    def start_stage(k):
        copies = []
        for part in range(KV_PARTS):
            copy = send(
                part_ref.at[pl.ds(2**k, 2**k), part],
                lands[k].at[pl.ds(0, 2**k), part],
                send_sem.at[k, part],
                recv_sem.at[k, part],
                peers[(part + k) % 4],
            )
            copy.start()
            copies.append(copy)
        return copies

    def finish_stage(k, copies):
        for copy in copies:
            copy.wait()

        def add(p, carry):
            part_ref[p] = part_ref[p] + lands[k][p]
            return carry

        lax.fori_loop(0, 2**k, add, 0)

    lax.fori_loop(8, 16, one_place, 0)
    copies = start_stage(3)
    lax.fori_loop(0, 8, one_place, 0)
    finish_stage(3, copies)
    for k in (2, 1, 0):
        finish_stage(k, start_stage(k))
    zcopies = []
    for part in range(KV_PARTS):
        copy = send(
            part_ref.at[0, part, pl.ds(KV_ROWS, KV_ROWS)],
            landz.at[part],
            zsend_sem.at[part],
            zrecv_sem.at[part],
            peers[4],
        )
        copy.start()
        zcopies.append(copy)
    for head in range(MEMBERS):
        grad = dq_acc[head * TOK : (head + 1) * TOK] * (1.0 / math.sqrt(HEAD))
        dq_ref[:, head * HEAD : (head + 1) * HEAD] = grad.astype(jnp.bfloat16)
    for part in range(KV_PARTS):
        zcopies[part].wait()
        dkv_ref[part * KV_ROWS : (part + 1) * KV_ROWS] = part_ref[0, part, 0:KV_ROWS] + landz[part]


def backward_attention(kbase, queries, back_attended, held, qpos, slopes, lse, delta):
    vmem = pl.BlockSpec(memory_space=pltpu.VMEM)
    block = (KV_PARTS, 2 * KV_ROWS, 2 * HEAD)
    return pl.pallas_call(
        backward_kernel,
        out_shape=(
            jax.ShapeDtypeStruct((TOK, QW), jnp.bfloat16),
            jax.ShapeDtypeStruct((TOK, 2 * HEAD), jnp.bfloat16),
        ),
        in_specs=[pl.BlockSpec(memory_space=pltpu.SMEM)] + [vmem] * 7,
        out_specs=(vmem, vmem),
        scratch_shapes=[
            pltpu.VMEM((MEMBERS * TOK, HEAD), jnp.bfloat16),
            pltpu.VMEM((MEMBERS * TOK, HEAD), jnp.bfloat16),
            pltpu.VMEM((MEMBERS * TOK, HEAD), jnp.float32),
            pltpu.VMEM((16,) + block, jnp.bfloat16),
            pltpu.VMEM((8,) + block, jnp.bfloat16),
            pltpu.VMEM((4,) + block, jnp.bfloat16),
            pltpu.VMEM((2,) + block, jnp.bfloat16),
            pltpu.VMEM((1,) + block, jnp.bfloat16),
            pltpu.VMEM((KV_PARTS, KV_ROWS, 2 * HEAD), jnp.bfloat16),
            pltpu.SemaphoreType.DMA((4, KV_PARTS)),
            pltpu.SemaphoreType.DMA((4, KV_PARTS)),
            pltpu.SemaphoreType.DMA((KV_PARTS,)),
            pltpu.SemaphoreType.DMA((KV_PARTS,)),
        ],
        compiler_params=pltpu.CompilerParams(
            collective_id=1, has_side_effects=True, vmem_limit_bytes=VMEM_LIMIT
        ),
    )(kbase, queries, back_attended, held, qpos, slopes, lse, delta)


PARTS = 5
CH = 48


def weights_kernel(
    normed_ref, cot_ref, win_ref, last_ref, patch_ref,
    dq_ref, att_ref, conv_ref, pair_ref, emb_ref,
    out_ref, other_ref,
    sums, land4, land3, land2, land1, land0, land_dp, land_tp, land_diag,
    send_sem, recv_sem, fsend_sem, frecv_sem,
    *, factor,
):
    seq, dp, tp = lax.axis_index("seq"), lax.axis_index("dp"), lax.axis_index("tp")
    peers = [{"seq": one_move(seq, d)} for d in range(5)]
    over = {"dp": 1 - dp}
    side = {"tp": 1 - tp}
    diagonal = {"dp": 1 - dp, "tp": 1 - tp}
    enter(peers + [over, side, diagonal])
    lands = [land0, land1, land2, land3, land4]
    first = lax.broadcasted_iota(jnp.int32, (4 * CH, QW // 2), 0) % CH < CH // 2

    def fill(part):
        def step(i, carry):
            group = 7 - i
            where = []
            for j in range(4):
                place = group * 4 + j
                bits = [(place // 2 ** ((d - part) % 5)) % 2 for d in range(5)]
                where.append(seq_peer(seq, bits))

            def rows(ref, start, count):
                return jnp.concatenate([ref[w, start : start + count] for w in where], axis=0)

            if part == 0:
                grads = dot_nn(rows(normed_ref, 0, CH), dq_ref[...])
            elif part == 1:
                grads = dot_nn(rows(cot_ref, 0, CH), att_ref[...])
            elif part < 4:
                grads = dot_nn(rows(win_ref, (part - 2) * CH, CH), conv_ref[...])
            else:
                wide = dot_nn(rows(last_ref, 0, CH), conv_ref[...])
                conv = jnp.where(first, wide[:, : QW // 2], wide[:, QW // 2 :])
                pair = dot_nn(rows(normed_ref, 0, CH), pair_ref[...])
                emb = dot_nn(rows(patch_ref, 0, 16), emb_ref[...])
                emb = jnp.concatenate(
                    [
                        emb[16 * j : 16 * j + 16, 128 * c : 128 * c + 128]
                        for j in range(4)
                        for c in range(3)
                    ],
                    axis=0,
                )
                grads = jnp.concatenate([conv, pair, emb], axis=1)
            sums[part, pl.ds(group * 4, 4)] = grads.astype(jnp.bfloat16).reshape(4, CH, QW)
            return carry

        return step

    def start(part, k):
        copies = []
        if k > 0:
            spans = ((2 ** (k - 1), 2 ** (k - 1)), (0, 2 ** (k - 1)))
        else:
            spans = ((0, 1),)
        for piece, (low, count) in enumerate(spans):
            copy = send(
                sums.at[part, pl.ds(2**k + low, count)],
                lands[k].at[part, pl.ds(low, count)],
                send_sem.at[part, k, piece],
                recv_sem.at[part, k, piece],
                peers[(part + k) % 5],
            )
            copy.start()
            copies.append((copy, low, count))
        return copies

    def settle(part, k, item):
        copy, low, count = item
        copy.wait()

        def add(i, carry):
            sums[part, low + i] = sums[part, low + i] + lands[k][part, low + i]
            return carry

        lax.fori_loop(0, count, add, 0)

    flights = []
    for part in range(PARTS):
        lax.fori_loop(0, 4, fill(part), 0)
        flights.append(start(part, 4))
    for part in range(PARTS):
        lax.fori_loop(4, 8, fill(part), 0)
    for k in (4, 3, 2, 1):
        after = []
        for part in range(PARTS):
            settle(part, k, flights[part][0])
            after.append(start(part, k - 1))
        for part in range(PARTS):
            settle(part, k, flights[part][1])
        flights = after
    finals = []
    for part in range(PARTS):
        settle(part, 0, flights[part][0])
        copy = send(
            sums.at[part, 0], land_dp.at[part], fsend_sem.at[part], frecv_sem.at[part], over
        )
        copy.start()
        finals.append(copy)
    emb_part = sums.at[4, 0, :, pl.ds(640, 128)]
    sidecopy = send(emb_part, land_tp, fsend_sem.at[5], frecv_sem.at[5], side)
    sidecopy.start()
    diagcopy = send(emb_part, land_diag, fsend_sem.at[6], frecv_sem.at[6], diagonal)
    diagcopy.start()
    for part in range(PARTS):
        finals[part].wait()
        total = sums[part, 0].astype(jnp.float32) + land_dp[part].astype(jnp.float32)
        out_ref[part] = total * factor
    sidecopy.wait()
    diagcopy.wait()
    total = land_tp[...].astype(jnp.float32) + land_diag[...].astype(jnp.float32)
    other_ref[...] = total * factor


def weight_gradients(factor, *operands):
    vmem = pl.BlockSpec(memory_space=pltpu.VMEM)
    return pl.pallas_call(
        functools.partial(weights_kernel, factor=factor),
        out_shape=(
            jax.ShapeDtypeStruct((PARTS, CH, QW), jnp.float32),
            jax.ShapeDtypeStruct((CH, HEAD), jnp.float32),
        ),
        in_specs=[vmem] * 10,
        out_specs=(vmem, vmem),
        scratch_shapes=[pltpu.VMEM((PARTS, 32, CH, QW), jnp.bfloat16)]
        + [pltpu.VMEM((PARTS, 2**k, CH, QW), jnp.bfloat16) for k in (4, 3, 2, 1, 0)]
        + [
            pltpu.VMEM((PARTS, CH, QW), jnp.bfloat16),
            pltpu.VMEM((CH, HEAD), jnp.bfloat16),
            pltpu.VMEM((CH, HEAD), jnp.bfloat16),
            pltpu.SemaphoreType.DMA((PARTS, 5, 2)),
            pltpu.SemaphoreType.DMA((PARTS, 5, 2)),
            pltpu.SemaphoreType.DMA((7,)),
            pltpu.SemaphoreType.DMA((7,)),
        ],
        compiler_params=pltpu.CompilerParams(
            collective_id=2, has_side_effects=True, vmem_limit_bytes=VMEM_LIMIT
        ),
    )(*operands)


def gelu_value(inputs):
    return (
        0.5 * inputs * (1.0 + jnp.tanh(ROOT_TWO_PI * (inputs + CUBIC * inputs * inputs * inputs)))
    )


def gelu_slope(inputs):
    inner = jnp.tanh(ROOT_TWO_PI * (inputs + CUBIC * inputs * inputs * inputs))
    return 0.5 * (1.0 + inner) + 0.5 * inputs * (1.0 - inner * inner) * ROOT_TWO_PI * (
        1.0 + 3.0 * CUBIC * inputs * inputs
    )


def inverse_rms(values):
    return lax.rsqrt(jnp.mean(values * values, axis=-1, keepdims=True) + EPSILON)


def unpack_local(packed, bases_tok):
    shift_bits = 2 * jnp.arange(16, dtype=jnp.int32)
    fields = jnp.right_shift(packed[:, None], shift_bits) & 3
    letters = fields.reshape(-1, bases_tok)
    onehot = letters[..., None] == jnp.arange(4, dtype=jnp.int32)
    return onehot.reshape(letters.shape[0], 4 * bases_tok).astype(jnp.bfloat16)


def sequence_rims(shard, width):
    size, length = lax.axis_size("seq"), shard.shape[0]
    up = [(i, (i + 1) % size) for i in range(size - 1)]
    down = [(j, i) for i, j in up]
    before = lax.ppermute(shard[length - width :], "seq", up)
    after = lax.ppermute(shard[:width], "seq", down)
    return jnp.concatenate([before, shard, after], axis=0)


def feature_halves(values):
    return lax.all_gather(values, "tp", axis=1, tiled=True)


def from_side(values):
    return lax.ppermute(values, "tp", [(0, 1), (1, 0)])


def per_device(
    bases,
    shifts,
    embed_weight,
    conv_weight,
    query_weight,
    keyvalue_weight,
    output_weight,
    slopes,
    cotangent,
):
    tokens = cotangent.shape[1]
    conv_in = embed_weight.shape[1]
    bases_tok = embed_weight.shape[0] // 4
    taps_count = conv_weight.shape[0]
    reach_rows = taps_count // 2
    local_out = conv_weight.shape[2]
    width_all = query_weight.shape[0]
    seq, tp = lax.axis_index("seq"), lax.axis_index("tp")
    seq_count = lax.axis_size("seq")

    patches = unpack_local(bases[0], bases_tok)
    embedded = jnp.dot(patches, embed_weight, preferred_element_type=jnp.float32).astype(
        jnp.bfloat16
    )
    embedded_wide = embedded.astype(jnp.float32)
    scale_in = inverse_rms(embedded_wide)
    normed_in = embedded_wide * scale_in
    activated = gelu_value(normed_in).astype(jnp.bfloat16)
    padded = sequence_rims(activated, reach_rows)
    windows = jnp.concatenate(
        [padded[tap_index : tap_index + tokens] for tap_index in range(taps_count)], axis=-1
    )
    convolved = jnp.dot(
        windows,
        conv_weight.reshape(taps_count * conv_in, local_out),
        preferred_element_type=jnp.float32,
    )
    hidden = (convolved + embedded_wide).astype(jnp.bfloat16)
    hidden_full = feature_halves(hidden).astype(jnp.float32)
    scale_mid = inverse_rms(hidden_full)
    normed_wide = hidden_full * scale_mid
    normed = normed_wide.astype(jnp.bfloat16)
    queries = jnp.dot(normed, query_weight, preferred_element_type=jnp.float32).astype(jnp.bfloat16)
    pair_weight = keyvalue_weight.reshape(width_all, 2 * HEAD)
    keyvalue = jnp.dot(normed, pair_weight, preferred_element_type=jnp.float32).astype(jnp.bfloat16)

    cotangent_local = cotangent[0]
    cotangent_full = feature_halves(cotangent_local)
    back_attended = jnp.einsum(
        "tc,qc->tq", cotangent_full, output_weight, preferred_element_type=jnp.float32
    ).astype(jnp.bfloat16)

    token = jnp.arange(tokens, dtype=jnp.int32)
    qpos = (seq * tokens + token + shifts[0]).astype(jnp.float32)
    sources = jnp.bitwise_xor(seq, KV_MASKS) * tokens
    kbase = sources + (KV_ROWS * np.arange(KV_PARTS, dtype=np.int32))[None, :, None]
    kbase = kbase.reshape(16, 2 * KV_PARTS)
    kpos = kbase[:, :, None] + jnp.arange(KV_ROWS, dtype=jnp.int32)
    kpos = kpos.reshape(16, 1, 2 * tokens).astype(jnp.float32)
    attended, stats, held = forward_attention(
        slopes, queries, keyvalue, back_attended, qpos.reshape(tokens, 1), kpos
    )
    lse = stats[:, :MEMBERS].T.reshape(MEMBERS // 2, 1, 2 * tokens)
    delta = stats[:, 8 : 8 + MEMBERS].T.reshape(MEMBERS // 2, 1, 2 * tokens)

    partial_out = jnp.dot(attended, output_weight, preferred_element_type=jnp.float32).astype(
        jnp.bfloat16
    )
    halves = partial_out.reshape(tokens, 2, local_out)
    mine = jnp.where(tp == 0, halves[:, 0], halves[:, 1])
    yours = jnp.where(tp == 0, halves[:, 1], halves[:, 0])
    projected = mine.astype(jnp.float32) + from_side(yours).astype(jnp.float32)
    result = (hidden.astype(jnp.float32) + projected).astype(jnp.bfloat16)

    slope_rows = jnp.repeat(slopes * BIAS_SCALE, tokens).reshape(MEMBERS // 2, 1, 2 * tokens)
    back_query, back_pair = backward_attention(
        kbase.astype(jnp.float32),
        queries,
        back_attended,
        held,
        jnp.tile(qpos, 2).reshape(1, 2 * tokens),
        slope_rows,
        lse,
        delta,
    )

    normed_partial = jnp.einsum(
        "tq,cq->tc", back_query, query_weight, preferred_element_type=jnp.float32
    )
    normed_partial = normed_partial + jnp.einsum(
        "tq,cq->tc", back_pair, pair_weight, preferred_element_type=jnp.float32
    )
    normed_partial = normed_partial.astype(jnp.bfloat16)
    back_normed = normed_partial.astype(jnp.float32) + from_side(normed_partial).astype(jnp.float32)
    back_wide = scale_mid * (
        back_normed - normed_wide * jnp.mean(back_normed * normed_wide, axis=-1, keepdims=True)
    )
    back_hidden = cotangent_local.astype(jnp.float32) + lax.dynamic_slice_in_dim(
        back_wide, tp * local_out, local_out, 1
    )
    back_conv = back_hidden.astype(jnp.bfloat16)
    back_padded = sequence_rims(back_conv, reach_rows)
    back_windows = jnp.concatenate(
        [
            back_padded[taps_count - 1 - tap_index : taps_count - 1 - tap_index + tokens]
            for tap_index in range(taps_count)
        ],
        axis=-1,
    )
    active_partial = jnp.einsum(
        "tko,kco->tc",
        back_windows.reshape(tokens, taps_count, local_out),
        conv_weight,
        preferred_element_type=jnp.float32,
    ).astype(jnp.bfloat16)
    ours = jnp.concatenate([active_partial, back_conv], axis=1)
    summed = ours.astype(jnp.float32) + from_side(ours).astype(jnp.float32)
    back_active, back_residual = summed[:, :conv_in], summed[:, conv_in:]
    back_normed_in = back_active * gelu_slope(normed_in)
    back_embedded = back_residual + scale_in * (
        back_normed_in - normed_in * jnp.mean(back_normed_in * normed_in, axis=-1, keepdims=True)
    )
    back_embedded = back_embedded.astype(jnp.bfloat16)
    half = conv_in // 2
    emb_half = jnp.where(tp == 0, back_embedded[:, :half], back_embedded[:, half:])

    rows = conv_in // seq_count
    by_chunk = windows.reshape(tokens, taps_count, seq_count, rows).transpose(2, 1, 3, 0)
    early = by_chunk[:, :4].reshape(seq_count, 4 * rows, tokens)
    last = jnp.concatenate([by_chunk[:, 4], by_chunk[:, 4]], axis=1)
    factor = (lax.axis_size("dp") * seq_count * tokens) ** (-0.5)
    sums, other = weight_gradients(
        factor,
        normed.T.reshape(seq_count, CH, tokens),
        cotangent_full.T.reshape(seq_count, CH, tokens),
        early,
        last,
        patches.T.reshape(seq_count, 16, tokens),
        back_query,
        attended,
        back_conv,
        back_pair,
        emb_half,
    )
    grad_query = sums[0]
    grad_output = sums[1].T
    tail = sums[4, :, :half]
    tail = jnp.concatenate([tail[:rows], tail[rows:]], axis=1)
    grad_conv = jnp.concatenate([sums[2:4].reshape(4, rows, local_out), tail[None]], axis=0)
    grad_pair = sums[4, :, half : half + 2 * HEAD].reshape(CH, 1, 2 * HEAD)

    def embed_rows(block):
        return jnp.concatenate([block[:16], block[16:32], block[32:]], axis=1)

    own, others = embed_rows(sums[4, :, half + 2 * HEAD :]), embed_rows(other)
    grad_embed = jnp.concatenate(
        [jnp.where(tp == 0, own, others), jnp.where(tp == 0, others, own)], axis=1
    )
    return (result[None], grad_embed, grad_conv, grad_query, grad_pair, grad_output)


def solution(mesh):
    placed = (
        P("dp", "seq"),
        P("dp"),
        P(),
        P(None, None, "tp"),
        P(None, "tp"),
        P(None, "tp", None),
        P("tp", None),
        P("tp"),
        P("dp", "seq", "tp"),
    )
    return jax.shard_map(
        per_device,
        mesh=mesh,
        in_specs=placed,
        out_specs=(
            P("dp", "seq", "tp"),
            P("seq", None),
            P(None, "seq", "tp"),
            P("seq", "tp"),
            P("seq", "tp", None),
            P("tp", "seq"),
        ),
        check_vma=False,
    )
```

```python
import functools
import math

import jax
import jax.numpy as jnp
import numpy as np
from jax import lax
from jax.experimental import pallas as pl
from jax.experimental.pallas import tpu as pltpu
from jax.sharding import PartitionSpec as P

ROOT_TWO_PI = math.sqrt(2.0 / math.pi)
CUBIC = 0.044715
EPSILON = 1e-06
DISTANCE_SCALE = 128.0
MESH = pl.DeviceIdType.MESH
LOG2E = math.log2(math.e)
VMEM_LIMIT = 60 * 1024 * 1024

TOK = 192
HEAD = 128
MEMBERS = 6
QW = MEMBERS * HEAD
SCORE_SCALE = LOG2E / math.sqrt(HEAD)
BIAS_SCALE = LOG2E / DISTANCE_SCALE

KV_PARTS = 4
KV_ROWS = TOK // KV_PARTS


def flip(value, low, high):
    value = value + low * (1 - 2 * (value % 2))
    return value + high * (3 - 2 * value)


def seq_peer(seq, moves):
    y, x, z = seq // 8, (seq // 2) % 4, seq % 2
    y = flip(y, moves[2], moves[3])
    x = flip(x, moves[0], moves[1])
    z = z + moves[4] * (1 - 2 * z)
    return (y * 4 + x) * 2 + z


def one_move(seq, direction):
    return seq_peer(seq, [1 if d == direction else 0 for d in range(5)])


def kv_mask(part, place, z):
    bits = [(place >> ((d - part) % 4)) & 1 for d in range(4)]
    x = bits[0] ^ (3 * bits[1])
    y = bits[2] ^ (3 * bits[3])
    return (y << 3) | (x << 1) | z


KV_MASKS = np.array(
    [[[kv_mask(q, p, z) for z in range(2)] for q in range(KV_PARTS)] for p in range(16)], np.int32
)


def enter(peers):
    barrier = pltpu.get_barrier_semaphore()
    for peer in peers:
        pl.semaphore_signal(barrier, inc=1, device_id=peer, device_id_type=MESH)
    pl.semaphore_wait(barrier, len(peers))


def send(src, dst, send_sem, recv_sem, peer):
    return pltpu.make_async_remote_copy(
        src_ref=src,
        dst_ref=dst,
        send_sem=send_sem,
        recv_sem=recv_sem,
        device_id=peer,
        device_id_type=MESH,
    )


NT = (((1,), (1,)), ((), ()))
TN = (((0,), (0,)), ((), ()))


def dot_nt(a, b):
    return lax.dot_general(a, b, NT, preferred_element_type=jnp.float32)


def dot_tn(a, b):
    return lax.dot_general(a, b, TN, preferred_element_type=jnp.float32)


def dot_nn(a, b):
    return jnp.dot(a, b, preferred_element_type=jnp.float32)


EDGE = 16
CH = 48


def gelu_value(inputs):
    return (
        0.5 * inputs * (1.0 + jnp.tanh(ROOT_TWO_PI * (inputs + CUBIC * inputs * inputs * inputs)))
    )


def gelu_slope(inputs):
    inner = jnp.tanh(ROOT_TWO_PI * (inputs + CUBIC * inputs * inputs * inputs))
    return 0.5 * (1.0 + inner) + 0.5 * inputs * (1.0 - inner * inner) * ROOT_TWO_PI * (
        1.0 + 3.0 * CUBIC * inputs * inputs
    )


def inverse_rms(values):
    return lax.rsqrt(jnp.mean(values * values, axis=-1, keepdims=True) + EPSILON)


def unpack_bases(words):
    lane = lax.broadcasted_iota(jnp.int32, (TOK, HEAD), 1)
    shift, letter = 2 * ((lane // 4) % 16), lane % 4
    blocks = []
    for j in range(4):
        word = jnp.where(lane < 64, words[:, 2 * j : 2 * j + 1], words[:, 2 * j + 1 : 2 * j + 2])
        field = jnp.bitwise_and(jnp.right_shift(word, shift), 3)
        blocks.append((field == letter).astype(jnp.float32))
    return jnp.concatenate(blocks, axis=1)


def halo(edge_ref, sems, seq):
    after = {"seq": (seq + 1) % 32}
    before = {"seq": (seq + 31) % 32}
    (send_a, recv_a), (send_b, recv_b) = sems
    return [
        send(edge_ref.at[pl.ds(TOK, EDGE)], edge_ref.at[pl.ds(0, EDGE)], send_a, recv_a, after),
        send(
            edge_ref.at[pl.ds(EDGE, EDGE)],
            edge_ref.at[pl.ds(EDGE + TOK, EDGE)],
            send_b,
            recv_b,
            before,
        ),
    ]


def with_edges(edge_ref, seq):
    blank = jnp.zeros((EDGE, QW), jnp.bfloat16)
    head_rows = jnp.where(seq > 0, edge_ref[0:EDGE], blank)
    tail_rows = jnp.where(seq < 31, edge_ref[EDGE + TOK :], blank)
    return jnp.concatenate([head_rows, edge_ref[EDGE : EDGE + TOK], tail_rows], axis=0)


def forward_kernel(
    slope_ref, words_ref, emb_w_ref, cot_ref, qpos_ref, kpos_ref, cw_hbm, qw_hbm, kvw_hbm, ow_hbm,
    att_ref, stat_ref, held_ref, q_ref, back_ref, hidden_ref, embedded_ref, edge_ref,
    normed_t_ref, cot_t_ref,
    cw_ref, qw_ref, kvw_ref, ow_ref, cot_full, kv_ref, normed_ref, acc_ref, top_ref,
    load_sem, send_sem, recv_sem, zsend_sem, zrecv_sem, msend_sem, mrecv_sem,
):
    seq, tp = lax.axis_index("seq"), lax.axis_index("tp")
    loads = []
    for i, (far, near) in enumerate(
        ((ow_hbm, ow_ref), (cw_hbm, cw_ref), (qw_hbm, qw_ref), (kvw_hbm, kvw_ref))
    ):
        loads.append(pltpu.make_async_copy(far, near, load_sem.at[i]))
        loads[i].start()
    peers = [{"seq": one_move(seq, d)} for d in range(5)]
    side = {"tp": 1 - tp}
    enter(peers + [side, {"seq": (seq + 1) % 32}, {"seq": (seq + 31) % 32}])
    mine = pl.ds(pl.multiple_of(tp * QW, HEAD), QW)
    cot_copy = send(cot_ref, cot_full.at[:, mine], msend_sem.at[0], mrecv_sem.at[0], side)
    cot_copy.start()
    patches = unpack_bases(words_ref[...]).astype(jnp.bfloat16)
    embedded = dot_nn(patches, emb_w_ref[...]).astype(jnp.bfloat16)
    embedded_ref[...] = embedded
    embedded_wide = embedded.astype(jnp.float32)
    activated = gelu_value(embedded_wide * inverse_rms(embedded_wide))
    edge_ref[EDGE : EDGE + TOK] = activated.astype(jnp.bfloat16)
    edges = halo(
        edge_ref,
        ((msend_sem.at[1], mrecv_sem.at[1]), (msend_sem.at[2], mrecv_sem.at[2])),
        seq,
    )
    for copy in edges:
        copy.start()
    cot_full[:, mine] = cot_ref[...]
    cot_copy.wait()
    loads[0].wait()
    back_ref[...] = dot_nt(cot_full[...], ow_ref[...]).astype(jnp.bfloat16)
    for copy in edges:
        copy.wait()
    loads[1].wait()
    padded = with_edges(edge_ref, seq)
    hidden = embedded_ref[...].astype(jnp.float32)
    for tap in range(5):
        moved = dot_nn(padded, cw_ref[tap])
        hidden = hidden + moved[EDGE - 2 + tap : EDGE - 2 + tap + TOK]
    hidden_ref[:, mine] = hidden.astype(jnp.bfloat16)
    hidden_copy = send(
        hidden_ref.at[:, mine], hidden_ref.at[:, mine], msend_sem.at[3], mrecv_sem.at[3], side
    )
    hidden_copy.start()
    acc_ref[...] = jnp.zeros_like(acc_ref)
    top_ref[...] = jnp.full_like(top_ref, -1e30)
    hidden_copy.wait()
    loads[2].wait()
    loads[3].wait()
    hidden_wide = hidden_ref[...].astype(jnp.float32)
    normed_ref[...] = (hidden_wide * inverse_rms(hidden_wide)).astype(jnp.bfloat16)
    kv_ref[...] = dot_nn(normed_ref[...], kvw_ref[...]).astype(jnp.bfloat16)
    zcopies = []
    for part in range(KV_PARTS):
        rows = pl.ds(part * KV_ROWS, KV_ROWS)
        copy = send(
            kv_ref.at[rows],
            held_ref.at[0, part, pl.ds(KV_ROWS, KV_ROWS)],
            zsend_sem.at[part],
            zrecv_sem.at[part],
            peers[4],
        )
        copy.start()
        zcopies.append(copy)
    for part in range(KV_PARTS):
        held_ref[0, part, 0:KV_ROWS] = kv_ref[part * KV_ROWS : (part + 1) * KV_ROWS]
    q_ref[...] = dot_nn(normed_ref[...], qw_ref[...]).astype(jnp.bfloat16)
    qpos = qpos_ref[...]

    def absorb(pair, kpos):
        keys = pair[:, :HEAD]
        values = jnp.concatenate([pair[:, HEAD:], jnp.ones_like(keys)], axis=1)
        distance = jnp.abs(qpos - kpos)
        for head in range(MEMBERS):
            scores = dot_nt(q_ref[:, head * HEAD : (head + 1) * HEAD], keys) * SCORE_SCALE
            scores = scores - distance * (slope_ref[head] * BIAS_SCALE)
            old = top_ref[head]
            new = jnp.maximum(old, jnp.max(scores, axis=1, keepdims=True))
            fading = jnp.exp2(old - new)
            weights = jnp.exp2(scores - new[:, :1]).astype(jnp.bfloat16)
            acc_ref[head] = acc_ref[head] * jnp.concatenate([fading, fading], axis=1) + dot_nn(
                weights, values
            )
            top_ref[head] = new

    def places(first, count):
        pair = held_ref[pl.ds(first, count)].reshape(count * 2 * TOK, 2 * HEAD)
        if count == 1:
            kpos = kpos_ref[first]
        else:
            kpos = jnp.concatenate([kpos_ref[first + i] for i in range(count)], axis=1)
        absorb(pair, kpos)

    def start_stage(k):
        copies = []
        for part in range(KV_PARTS):
            copy = send(
                held_ref.at[pl.ds(0, 2**k), part],
                held_ref.at[pl.ds(2**k, 2**k), part],
                send_sem.at[k, part],
                recv_sem.at[k, part],
                peers[(part + k) % 4],
            )
            copy.start()
            copies.append(copy)
        return copies

    def turned(ref, target, first, count):
        columns = slice(first * 2 * CH * 4, (first + count) * 2 * CH * 4)
        block = ref[:, columns].astype(jnp.float32).T.astype(jnp.bfloat16)
        target[8 * first : 8 * (first + count)] = block.reshape(8 * count, CH, TOK)

    for copy in zcopies:
        copy.wait()
    stage = start_stage(0)
    places(0, 1)
    for copy in stage:
        copy.wait()
    stage = start_stage(1)
    places(1, 1)
    turned(normed_ref, normed_t_ref, 0, 1)
    for copy in stage:
        copy.wait()
    stage = start_stage(2)
    places(2, 2)
    turned(normed_ref, normed_t_ref, 1, 2)
    for copy in stage:
        copy.wait()
    stage = start_stage(3)

    def two_places(first):
        def step(i, carry):
            places(first + 2 * i, 2)
            return carry

        return step

    lax.fori_loop(0, 2, two_places(4), 0)
    turned(normed_ref, normed_t_ref, 3, 1)
    turned(cot_full, cot_t_ref, 0, 4)
    for copy in stage:
        copy.wait()
    lax.fori_loop(0, 4, two_places(8), 0)
    lane = lax.broadcasted_iota(jnp.int32, (TOK, HEAD), 1)
    stats = jnp.zeros((TOK, HEAD), jnp.float32)
    for head in range(MEMBERS):
        totals = acc_ref[head, :, HEAD:]
        mixed = (acc_ref[head, :, :HEAD] / totals).astype(jnp.bfloat16)
        att_ref[:, head * HEAD : (head + 1) * HEAD] = mixed
        back = back_ref[:, head * HEAD : (head + 1) * HEAD].astype(jnp.float32)
        delta = jnp.sum(back * mixed.astype(jnp.float32), axis=1, keepdims=True)
        stats = jnp.where(lane == head, top_ref[head] + jnp.log2(totals), stats)
        stats = jnp.where(lane == 8 + head, delta, stats)
    stat_ref[...] = stats


def forward_attention(*operands):
    vmem = pl.BlockSpec(memory_space=pltpu.VMEM)
    f32, bf16 = jnp.float32, jnp.bfloat16
    return pl.pallas_call(
        forward_kernel,
        out_shape=(
            jax.ShapeDtypeStruct((TOK, QW), bf16),
            jax.ShapeDtypeStruct((TOK, HEAD), f32),
            jax.ShapeDtypeStruct((16, KV_PARTS, 2 * KV_ROWS, 2 * HEAD), bf16),
            jax.ShapeDtypeStruct((TOK, QW), bf16),
            jax.ShapeDtypeStruct((TOK, QW), bf16),
            jax.ShapeDtypeStruct((TOK, 2 * QW), bf16),
            jax.ShapeDtypeStruct((TOK, QW), bf16),
            jax.ShapeDtypeStruct((TOK + 2 * EDGE, QW), bf16),
            jax.ShapeDtypeStruct((32, CH, TOK), bf16),
            jax.ShapeDtypeStruct((32, CH, TOK), bf16),
        ),
        in_specs=[pl.BlockSpec(memory_space=pltpu.SMEM)]
        + [vmem] * 5
        + [pl.BlockSpec(memory_space=pl.ANY)] * 4,
        out_specs=(vmem,) * 10,
        scratch_shapes=[
            pltpu.VMEM((5, QW, QW), bf16),
            pltpu.VMEM((2 * QW, QW), bf16),
            pltpu.VMEM((2 * QW, 2 * HEAD), bf16),
            pltpu.VMEM((QW, 2 * QW), bf16),
            pltpu.VMEM((TOK, 2 * QW), bf16),
            pltpu.VMEM((TOK, 2 * HEAD), bf16),
            pltpu.VMEM((TOK, 2 * QW), bf16),
            pltpu.VMEM((MEMBERS, TOK, 2 * HEAD), f32),
            pltpu.VMEM((MEMBERS, TOK, HEAD), f32),
            pltpu.SemaphoreType.DMA((4,)),
            pltpu.SemaphoreType.DMA((4, KV_PARTS)),
            pltpu.SemaphoreType.DMA((4, KV_PARTS)),
            pltpu.SemaphoreType.DMA((KV_PARTS,)),
            pltpu.SemaphoreType.DMA((KV_PARTS,)),
            pltpu.SemaphoreType.DMA((4,)),
            pltpu.SemaphoreType.DMA((4,)),
        ],
        compiler_params=pltpu.CompilerParams(
            collective_id=0, has_side_effects=True, vmem_limit_bytes=VMEM_LIMIT
        ),
    )(*operands)


def backward_kernel(
    kbase_ref, q_ref, back_ref, held_ref, qpos_ref, slope_ref, lse_ref, delta_ref,
    dq_ref, dkv_ref,
    qs_ref, bs_ref, dq_acc, part_ref, land3, land2, land1, land0, landz,
    send_sem, recv_sem, zsend_sem, zrecv_sem,
):
    seq = lax.axis_index("seq")
    peers = [{"seq": one_move(seq, d)} for d in range(5)]
    enter(peers)
    lands = [land0, land1, land2, land3]
    for head in range(MEMBERS):
        rows = slice(head * TOK, (head + 1) * TOK)
        qs_ref[rows] = q_ref[:, head * HEAD : (head + 1) * HEAD]
        bs_ref[rows] = back_ref[:, head * HEAD : (head + 1) * HEAD]
    dq_acc[...] = jnp.zeros_like(dq_acc)
    qpos = qpos_ref[...]
    row = lax.broadcasted_iota(jnp.int32, (KV_ROWS, 1), 0).astype(jnp.float32)

    def one_place(place, carry):
        pair = held_ref[place].reshape(2 * TOK, 2 * HEAD)
        keys, values = pair[:, :HEAD], pair[:, HEAD:]
        kpos = jnp.concatenate([row + kbase_ref[place, g] for g in range(8)], axis=0)
        distance = jnp.abs(qpos - kpos)
        key_grad = jnp.zeros((2 * TOK, HEAD), jnp.float32)
        value_grad = jnp.zeros((2 * TOK, HEAD), jnp.float32)
        for duo in range(MEMBERS // 2):
            rows = slice(duo * 2 * TOK, (duo + 1) * 2 * TOK)
            qd, bd = qs_ref[rows], bs_ref[rows]
            scores = dot_nt(keys, qd) * SCORE_SCALE - distance * slope_ref[duo]
            probs = jnp.exp2(scores - lse_ref[duo])
            back_probs = dot_nt(values, bd)
            grad_scores = (probs * (back_probs - delta_ref[duo])).astype(jnp.bfloat16)
            value_grad = value_grad + dot_nn(probs.astype(jnp.bfloat16), bd)
            key_grad = key_grad + dot_nn(grad_scores, qd)
            dq_acc[rows] += dot_tn(grad_scores, keys)
        both = jnp.concatenate([key_grad * (1.0 / math.sqrt(HEAD)), value_grad], axis=1)
        part_ref[place] = both.astype(jnp.bfloat16).reshape(KV_PARTS, 2 * KV_ROWS, 2 * HEAD)
        return carry

    def start_stage(k):
        copies = []
        for part in range(KV_PARTS):
            copy = send(
                part_ref.at[pl.ds(2**k, 2**k), part],
                lands[k].at[pl.ds(0, 2**k), part],
                send_sem.at[k, part],
                recv_sem.at[k, part],
                peers[(part + k) % 4],
            )
            copy.start()
            copies.append(copy)
        return copies

    def take_in(low, high, copies, stage):
        for copy in copies:
            copy.wait()

        def add(p, carry):
            total = part_ref[p].astype(jnp.float32)
            for k in range(stage, 4):
                total = total + lands[k][p].astype(jnp.float32)
            part_ref[p] = total.astype(jnp.bfloat16)
            return carry

        lax.fori_loop(low, high, add, 0)

    lax.fori_loop(8, 16, one_place, 0)
    copies = start_stage(3)
    for k in (2, 1, 0):
        lax.fori_loop(2**k, 2 ** (k + 1), one_place, 0)
        take_in(2**k, 2 ** (k + 1), copies, k + 1)
        copies = start_stage(k)
    lax.fori_loop(0, 1, one_place, 0)
    take_in(0, 1, copies, 0)
    zcopies = []
    for part in range(KV_PARTS):
        copy = send(
            part_ref.at[0, part, pl.ds(KV_ROWS, KV_ROWS)],
            landz.at[part],
            zsend_sem.at[part],
            zrecv_sem.at[part],
            peers[4],
        )
        copy.start()
        zcopies.append(copy)
    for head in range(MEMBERS):
        grad = dq_acc[head * TOK : (head + 1) * TOK] * (1.0 / math.sqrt(HEAD))
        dq_ref[:, head * HEAD : (head + 1) * HEAD] = grad.astype(jnp.bfloat16)
    for part in range(KV_PARTS):
        zcopies[part].wait()
        dkv_ref[part * KV_ROWS : (part + 1) * KV_ROWS] = part_ref[0, part, 0:KV_ROWS] + landz[part]


def backward_attention(kbase, queries, back_attended, held, qpos, slopes, lse, delta):
    vmem = pl.BlockSpec(memory_space=pltpu.VMEM)
    block = (KV_PARTS, 2 * KV_ROWS, 2 * HEAD)
    return pl.pallas_call(
        backward_kernel,
        out_shape=(
            jax.ShapeDtypeStruct((TOK, QW), jnp.bfloat16),
            jax.ShapeDtypeStruct((TOK, 2 * HEAD), jnp.bfloat16),
        ),
        in_specs=[pl.BlockSpec(memory_space=pltpu.SMEM)] + [vmem] * 7,
        out_specs=(vmem, vmem),
        scratch_shapes=[
            pltpu.VMEM((MEMBERS * TOK, HEAD), jnp.bfloat16),
            pltpu.VMEM((MEMBERS * TOK, HEAD), jnp.bfloat16),
            pltpu.VMEM((MEMBERS * TOK, HEAD), jnp.float32),
            pltpu.VMEM((16,) + block, jnp.bfloat16),
            pltpu.VMEM((8,) + block, jnp.bfloat16),
            pltpu.VMEM((4,) + block, jnp.bfloat16),
            pltpu.VMEM((2,) + block, jnp.bfloat16),
            pltpu.VMEM((1,) + block, jnp.bfloat16),
            pltpu.VMEM((KV_PARTS, KV_ROWS, 2 * HEAD), jnp.bfloat16),
            pltpu.SemaphoreType.DMA((4, KV_PARTS)),
            pltpu.SemaphoreType.DMA((4, KV_PARTS)),
            pltpu.SemaphoreType.DMA((KV_PARTS,)),
            pltpu.SemaphoreType.DMA((KV_PARTS,)),
        ],
        compiler_params=pltpu.CompilerParams(
            collective_id=1, has_side_effects=True, vmem_limit_bytes=VMEM_LIMIT
        ),
    )(kbase, queries, back_attended, held, qpos, slopes, lse, delta)


HALF = QW // 2
WIDTHS = (HALF, HALF, HALF, HALF, 2 * HEAD, HALF, HALF, HALF, HALF, HALF, HEAD)
TURNS = (2, 3, 0, 1, 4, 0, 1, 2, 3, 4, 4)
EARLY = (2, 3, 0, 1, 4)
LATE = (5, 6, 7, 8, 9)
EMBED = 10

def weights_kernel(
    normed_ref, cot_ref, act_ref, words_ref,
    dq_ref, att_ref, pair_ref, hidden_ref, embedded_ref, cotangent_ref,
    cw_hbm, qw_hbm, kvw_hbm, ow_hbm,
    result_out, query_out, output_out, pair_out, conv_out, embed_out,
    *scratch, factor,
):
    sums, lands, dp_lands = scratch[:11], scratch[11:22], scratch[22:33]
    (
        cw_ref, qw_ref, kvw_ref, ow_ref, win_ref, patch_ref, out_own, out_side,
        wide_own, wide_side, edge_ref, conv_side, active_own, active_side, emb_ref,
        land_tp, land_diag, load_sem, send_sem, recv_sem, fsend_sem, frecv_sem,
    ) = scratch[33:]
    seq, dp, tp = lax.axis_index("seq"), lax.axis_index("dp"), lax.axis_index("tp")
    loads = []
    for i, (far, near) in enumerate(
        ((qw_hbm, qw_ref), (kvw_hbm, kvw_ref), (ow_hbm, ow_ref), (cw_hbm, cw_ref))
    ):
        loads.append(pltpu.make_async_copy(far, near, load_sem.at[i]))
        loads[i].start()
    peers = [{"seq": one_move(seq, d)} for d in range(5)]
    over = {"dp": 1 - dp}
    side = {"tp": 1 - tp}
    diagonal = {"dp": 1 - dp, "tp": 1 - tp}
    around = [{"seq": (seq + 1) % 32}, {"seq": (seq + 31) % 32}]
    enter(peers + [over, side, diagonal] + around)
    upper = lax.broadcasted_iota(jnp.int32, (16 * CH, HALF), 0) % CH < CH // 2

    def fill(part, half):
        turn = TURNS[part]
        where = []
        for place in range(16 * half, 16 * half + 16):
            bits = [(place >> ((d - turn) % 5)) & 1 for d in range(5)]
            where.append(seq_peer(seq, bits))

        def rows(ref, start, count):
            return jnp.concatenate([ref[w, start : start + count] for w in where], axis=0)

        conv = slice(EDGE, EDGE + TOK)
        if part < 2:
            grads = dot_nn(rows(normed_ref, 0, CH), dq_ref[:, part * HALF : (part + 1) * HALF])
        elif part < 4:
            columns = slice((part - 2) * HALF, (part - 1) * HALF)
            grads = dot_nn(rows(cot_ref, 0, CH), att_ref[:, columns])
        elif part == 4:
            grads = dot_nn(rows(normed_ref, 0, CH), pair_ref[...])
        elif part < 9:
            column = (part - 5) % 2 * HALF
            chosen = rows(win_ref.at[(part - 5) // 2], 0, CH)
            grads = dot_nn(chosen, edge_ref[conv, column : column + HALF])
        elif part == 9:
            chosen = rows(win_ref.at[2], 0, CH)
            left = dot_nn(chosen, edge_ref[conv, :HALF])
            grads = jnp.where(upper, left, dot_nn(chosen, edge_ref[conv, HALF:]))
        else:
            columns = pl.ds(pl.multiple_of(tp * HALF, HEAD), HALF)
            emb = dot_nn(rows(patch_ref, 0, 16), emb_ref[:, columns])
            grads = jnp.concatenate(
                [
                    emb[16 * j : 16 * j + 16, HEAD * c : HEAD * c + HEAD]
                    for j in range(16)
                    for c in range(3)
                ],
                axis=0,
            )
        sums[part][16 * half : 16 * half + 16] = grads.astype(jnp.bfloat16).reshape(
            16, CH, WIDTHS[part]
        )

    def start(part, k):
        copies = []
        if k > 0:
            spans = ((2 ** (k - 1), 2 ** (k - 1)), (0, 2 ** (k - 1)))
        else:
            spans = ((0, 1),)
        for piece, (low, count) in enumerate(spans):
            copy = send(
                sums[part].at[pl.ds(2**k + low, count)],
                lands[part].at[pl.ds(2**k + low, count)],
                send_sem.at[part, k, piece],
                recv_sem.at[part, k, piece],
                peers[(TURNS[part] + k) % 5],
            )
            copy.start()
            copies.append((copy, low, count))
        return copies

    def settle(part, k, item):
        copy, low, count = item
        copy.wait()
        bunch = min(count, 4)

        def add(i, carry):
            at = pl.ds(low + i * bunch, bunch)
            sums[part][at] = sums[part][at] + lands[part][pl.ds(2**k + low + i * bunch, bunch)]
            return carry

        lax.fori_loop(0, count // bunch, add, 0)

    flights = {}

    def launch(parts):
        for part in parts:
            flights[part] = start(part, 4)

    def advance(parts, k):
        following = {}
        for part in parts:
            settle(part, k, flights[part][0])
            following[part] = start(part, k - 1)
        for part in parts:
            settle(part, k, flights[part][1])
        flights.update(following)

    finals = {}

    def finish(parts):
        for part in parts:
            settle(part, 0, flights[part][0])
            copy = send(
                sums[part].at[0], dp_lands[part], fsend_sem.at[part], frecv_sem.at[part], over
            )
            copy.start()
            finals[part] = copy

    def total(part):
        finals[part].wait()
        return (sums[part][0].astype(jnp.float32) + dp_lands[part][...].astype(jnp.float32)) * factor

    for part in EARLY:
        fill(part, 1)
        launch([part])
    loads[0].wait()
    loads[1].wait()
    partial = dot_nt(dq_ref[...], qw_ref[...]) + dot_nt(pair_ref[...], kvw_ref[...])
    wide_own[...] = partial.astype(jnp.bfloat16)
    wide_copy = send(wide_own, wide_side, fsend_sem.at[11], frecv_sem.at[11], side)
    wide_copy.start()
    padded = with_edges(act_ref, seq).astype(jnp.float32)
    turned = []
    for tap in range(5):
        window = padded[EDGE - 2 + tap : EDGE - 2 + tap + TOK].T
        turned.append(window.reshape(32, CH // 2, TOK))
    for i, pair in enumerate(((0, 1), (2, 3), (4, 4))):
        both = jnp.concatenate([turned[tap] for tap in pair], axis=1)
        win_ref[i] = both.astype(jnp.bfloat16)
    hidden = hidden_ref[...].astype(jnp.float32)
    scale = inverse_rms(hidden)
    wide_copy.wait()
    back_normed = wide_own[...].astype(jnp.float32) + wide_side[...].astype(jnp.float32)
    mean = jnp.mean(back_normed * (hidden * scale), axis=-1, keepdims=True)
    mine = pl.ds(pl.multiple_of(tp * QW, HEAD), QW)
    own = wide_own[:, mine].astype(jnp.float32) + wide_side[:, mine].astype(jnp.float32)
    normed = hidden_ref[:, mine].astype(jnp.float32) * scale
    back_hidden = cotangent_ref[...].astype(jnp.float32) + scale * (own - normed * mean)
    edge_ref[EDGE : EDGE + TOK] = back_hidden.astype(jnp.bfloat16)
    edge_copies = halo(
        edge_ref,
        ((fsend_sem.at[12], frecv_sem.at[12]), (fsend_sem.at[13], frecv_sem.at[13])),
        seq,
    )
    for copy in edge_copies:
        copy.start()
    conv_copy = send(
        edge_ref.at[pl.ds(EDGE, TOK)], conv_side, fsend_sem.at[14], frecv_sem.at[14], side
    )
    conv_copy.start()
    for part in LATE:
        fill(part, 1)
        launch([part])
    loads[3].wait()
    for copy in edge_copies:
        copy.wait()
    padded = with_edges(edge_ref, seq)
    active = jnp.zeros((TOK, QW), jnp.float32)
    for tap in range(5):
        moved = dot_nt(padded, cw_ref[tap])
        active = active + moved[EDGE + 2 - tap : EDGE + 2 - tap + TOK]
    active_own[...] = active.astype(jnp.bfloat16)
    active_copy = send(active_own, active_side, fsend_sem.at[15], frecv_sem.at[15], side)
    active_copy.start()
    loads[2].wait()
    out_own[...] = dot_nn(att_ref[...], ow_ref[...]).astype(jnp.bfloat16)
    theirs = pl.ds(pl.multiple_of((1 - tp) * QW, HEAD), QW)
    out_copy = send(out_own.at[:, theirs], out_side, fsend_sem.at[18], frecv_sem.at[18], side)
    out_copy.start()
    patches = unpack_bases(words_ref[...]).T
    patch_ref[...] = patches.reshape(32, 16, TOK).astype(jnp.bfloat16)
    embedded = embedded_ref[...].astype(jnp.float32)
    scale_in = inverse_rms(embedded)
    normed_in = embedded * scale_in
    slope = gelu_slope(normed_in)
    conv_copy.wait()
    residual = edge_ref[EDGE : EDGE + TOK].astype(jnp.float32) + conv_side[...].astype(jnp.float32)
    active_copy.wait()
    back_in = (active_own[...].astype(jnp.float32) + active_side[...].astype(jnp.float32)) * slope
    mean_in = jnp.mean(back_in * normed_in, axis=-1, keepdims=True)
    emb_ref[...] = (residual + scale_in * (back_in - normed_in * mean_in)).astype(jnp.bfloat16)
    fill(EMBED, 1)
    launch([EMBED])
    for part in EARLY + LATE + (EMBED,):
        fill(part, 0)
    out_copy.wait()
    projected = out_own[:, mine].astype(jnp.float32) + out_side[...].astype(jnp.float32)
    result_out[...] = (hidden_ref[:, mine].astype(jnp.float32) + projected).astype(jnp.bfloat16)
    late = LATE + (EMBED,)
    for k in (4, 3, 2, 1):
        advance(EARLY, k)
        advance(late, k)
    finish(EARLY)
    finish(late)
    sidecopy = send(sums[EMBED].at[0], land_tp, fsend_sem.at[16], frecv_sem.at[16], side)
    sidecopy.start()
    diagcopy = send(sums[EMBED].at[0], land_diag, fsend_sem.at[17], frecv_sem.at[17], diagonal)
    diagcopy.start()
    for half in range(2):
        query_out[:, half * HALF : (half + 1) * HALF] = total(half)
    for half in range(2):
        output_out[half * HALF : (half + 1) * HALF, :] = total(2 + half).T
    pair_out[...] = total(4)
    rows = CH // 2
    for part in range(4):
        tap, columns = part // 2 * 2, slice(part % 2 * HALF, (part % 2 + 1) * HALF)
        block = total(5 + part)
        conv_out[tap, :, columns] = block[:rows]
        conv_out[tap + 1, :, columns] = block[rows:]
    block = total(9)
    conv_out[4, :, :HALF] = block[:rows]
    conv_out[4, :, HALF:] = block[rows:]

    def embed_store(block, core):
        wide = jnp.concatenate([block[:16], block[16:32], block[32:]], axis=1)
        embed_out[:, pl.ds(pl.multiple_of(core * HALF, HEAD), HALF)] = wide

    embed_store(total(EMBED), tp)
    sidecopy.wait()
    diagcopy.wait()
    other = land_tp[...].astype(jnp.float32) + land_diag[...].astype(jnp.float32)
    embed_store(other * factor, 1 - tp)


def weight_gradients(factor, *operands):
    vmem = pl.BlockSpec(memory_space=pltpu.VMEM)
    f32, bf16 = jnp.float32, jnp.bfloat16
    return pl.pallas_call(
        functools.partial(weights_kernel, factor=factor),
        out_shape=(
            jax.ShapeDtypeStruct((TOK, QW), bf16),
            jax.ShapeDtypeStruct((CH, QW), f32),
            jax.ShapeDtypeStruct((QW, CH), f32),
            jax.ShapeDtypeStruct((CH, 2 * HEAD), f32),
            jax.ShapeDtypeStruct((5, CH // 2, QW), f32),
            jax.ShapeDtypeStruct((16, QW), f32),
        ),
        in_specs=[vmem] * 10 + [pl.BlockSpec(memory_space=pl.ANY)] * 4,
        out_specs=(vmem,) * 6,
        scratch_shapes=[pltpu.VMEM((32, CH, w), bf16) for w in WIDTHS]
        + [pltpu.VMEM((32, CH, w), bf16) for w in WIDTHS]
        + [pltpu.VMEM((CH, w), bf16) for w in WIDTHS]
        + [
            pltpu.VMEM((5, QW, QW), bf16),
            pltpu.VMEM((2 * QW, QW), bf16),
            pltpu.VMEM((2 * QW, 2 * HEAD), bf16),
            pltpu.VMEM((QW, 2 * QW), bf16),
            pltpu.VMEM((3, 32, CH, TOK), bf16),
            pltpu.VMEM((32, 16, TOK), bf16),
            pltpu.VMEM((TOK, 2 * QW), bf16),
            pltpu.VMEM((TOK, QW), bf16),
            pltpu.VMEM((TOK, 2 * QW), bf16),
            pltpu.VMEM((TOK, 2 * QW), bf16),
            pltpu.VMEM((TOK + 2 * EDGE, QW), bf16),
            pltpu.VMEM((TOK, QW), bf16),
            pltpu.VMEM((TOK, QW), bf16),
            pltpu.VMEM((TOK, QW), bf16),
            pltpu.VMEM((TOK, QW), bf16),
            pltpu.VMEM((CH, HEAD), bf16),
            pltpu.VMEM((CH, HEAD), bf16),
            pltpu.SemaphoreType.DMA((4,)),
            pltpu.SemaphoreType.DMA((11, 5, 2)),
            pltpu.SemaphoreType.DMA((11, 5, 2)),
            pltpu.SemaphoreType.DMA((19,)),
            pltpu.SemaphoreType.DMA((19,)),
        ],
        compiler_params=pltpu.CompilerParams(
            collective_id=2, has_side_effects=True, vmem_limit_bytes=VMEM_LIMIT
        ),
    )(*operands)


def per_device(
    bases,
    shifts,
    embed_weight,
    conv_weight,
    query_weight,
    keyvalue_weight,
    output_weight,
    slopes,
    cotangent,
):
    tokens = cotangent.shape[1]
    seq = lax.axis_index("seq")
    seq_count = lax.axis_size("seq")
    words = bases.reshape(tokens, -1)
    pair_weight = keyvalue_weight.reshape(2 * QW, 2 * HEAD)
    cotangent_local = cotangent[0]
    token = jnp.arange(tokens, dtype=jnp.int32)
    qpos = (seq * tokens + token + shifts[0]).astype(jnp.float32)
    sources = jnp.bitwise_xor(seq, KV_MASKS) * tokens
    kbase = sources + (KV_ROWS * np.arange(KV_PARTS, dtype=np.int32))[None, :, None]
    kbase = kbase.reshape(16, 2 * KV_PARTS)
    kpos = kbase[:, :, None] + jnp.arange(KV_ROWS, dtype=jnp.int32)
    kpos = kpos.reshape(16, 1, 2 * tokens).astype(jnp.float32)
    (
        attended, stats, held, queries, back_attended, hidden, embedded, edges, normed_t, cot_t
    ) = forward_attention(
        slopes,
        words,
        embed_weight,
        cotangent_local,
        qpos.reshape(tokens, 1),
        kpos,
        conv_weight,
        query_weight,
        pair_weight,
        output_weight,
    )
    lse = stats[:, :MEMBERS].T.reshape(MEMBERS // 2, 1, 2 * tokens)
    delta = stats[:, 8 : 8 + MEMBERS].T.reshape(MEMBERS // 2, 1, 2 * tokens)
    slope_rows = jnp.repeat(slopes * BIAS_SCALE, tokens).reshape(MEMBERS // 2, 1, 2 * tokens)
    back_query, back_pair = backward_attention(
        kbase.astype(jnp.float32),
        queries,
        back_attended,
        held,
        jnp.tile(qpos, 2).reshape(1, 2 * tokens),
        slope_rows,
        lse,
        delta,
    )
    factor = (lax.axis_size("dp") * seq_count * tokens) ** (-0.5)
    result, grad_query, grad_output, grad_pair, grad_conv, grad_embed = weight_gradients(
        factor,
        normed_t,
        cot_t,
        edges,
        words,
        back_query,
        attended,
        back_pair,
        hidden,
        embedded,
        cotangent_local,
        conv_weight,
        query_weight,
        pair_weight,
        output_weight,
    )
    grad_pair = grad_pair.reshape(CH, 1, 2 * HEAD)
    return (result[None], grad_embed, grad_conv, grad_query, grad_pair, grad_output)


def solution(mesh):
    placed = (
        P("dp", "seq"),
        P("dp"),
        P(),
        P(None, None, "tp"),
        P(None, "tp"),
        P(None, "tp", None),
        P("tp", None),
        P("tp"),
        P("dp", "seq", "tp"),
    )
    return jax.shard_map(
        per_device,
        mesh=mesh,
        in_specs=placed,
        out_specs=(
            P("dp", "seq", "tp"),
            P("seq", None),
            P(None, "seq", "tp"),
            P("seq", "tp"),
            P("seq", "tp", None),
            P("tp", "seq"),
        ),
        check_vma=False,
    )
```

```python
import functools
import math

import jax
import jax.numpy as jnp
from jax import lax
from jax.experimental import pallas as pl
from jax.experimental.pallas import tpu as pltpu
from jax.sharding import PartitionSpec as P

ROOT_TWO_PI = math.sqrt(2.0 / math.pi)
CUBIC = 0.044715
EPSILON = 1e-06
DISTANCE_SCALE = 128.0
MESH = pl.DeviceIdType.MESH
LOG2E = math.log2(math.e)
VMEM_LIMIT = 60 * 1024 * 1024

TOK = 192
HEAD = 128
MEMBERS = 6
QW = MEMBERS * HEAD
SCORE_SCALE = LOG2E / math.sqrt(HEAD)
BIAS_SCALE = LOG2E / DISTANCE_SCALE

KV_PARTS = 4
KV_ROWS = TOK // KV_PARTS


def flip(value, low, high):
    value = value + low * (1 - 2 * (value % 2))
    return value + high * (3 - 2 * value)


def seq_peer(seq, moves):
    y, x, z = seq // 8, (seq // 2) % 4, seq % 2
    y = flip(y, moves[2], moves[3])
    x = flip(x, moves[0], moves[1])
    z = z + moves[4] * (1 - 2 * z)
    return (y * 4 + x) * 2 + z


def one_move(seq, direction):
    return seq_peer(seq, [1 if d == direction else 0 for d in range(5)])


def pick(value):
    return [value, value + 1 - 2 * (value % 2), (value + 2) % 4, 3 - value]


def place_moves(part, place):
    return [(place // 2 ** ((d - part) % 4)) % 2 for d in range(4)]


def enter(peers):
    barrier = pltpu.get_barrier_semaphore()
    for peer in peers:
        pl.semaphore_signal(barrier, inc=1, device_id=peer, device_id_type=MESH)
    pl.semaphore_wait(barrier, len(peers))


def send(src, dst, send_sem, recv_sem, peer):
    return pltpu.make_async_remote_copy(
        src_ref=src,
        dst_ref=dst,
        send_sem=send_sem,
        recv_sem=recv_sem,
        device_id=peer,
        device_id_type=MESH,
    )


NT = (((1,), (1,)), ((), ()))
TN = (((0,), (0,)), ((), ()))


def dot_nt(a, b):
    return lax.dot_general(a, b, NT, preferred_element_type=jnp.float32)


def dot_tn(a, b):
    return lax.dot_general(a, b, TN, preferred_element_type=jnp.float32)


def dot_nn(a, b):
    return jnp.dot(a, b, preferred_element_type=jnp.float32)


EDGE = 16
CH = 48


def gelu_value(inputs):
    return (
        0.5 * inputs * (1.0 + jnp.tanh(ROOT_TWO_PI * (inputs + CUBIC * inputs * inputs * inputs)))
    )


def gelu_slope(inputs):
    inner = jnp.tanh(ROOT_TWO_PI * (inputs + CUBIC * inputs * inputs * inputs))
    return 0.5 * (1.0 + inner) + 0.5 * inputs * (1.0 - inner * inner) * ROOT_TWO_PI * (
        1.0 + 3.0 * CUBIC * inputs * inputs
    )


def inverse_rms(values):
    return lax.rsqrt(jnp.mean(values * values, axis=-1, keepdims=True) + EPSILON)


def unpack_bases(words):
    lane = lax.broadcasted_iota(jnp.int32, (TOK, HEAD), 1)
    shift, letter = 2 * ((lane // 4) % 16), lane % 4
    blocks = []
    for j in range(4):
        word = jnp.where(lane < 64, words[:, 2 * j : 2 * j + 1], words[:, 2 * j + 1 : 2 * j + 2])
        field = jnp.bitwise_and(jnp.right_shift(word, shift), 3)
        blocks.append((field == letter).astype(jnp.float32))
    return jnp.concatenate(blocks, axis=1)


def halo(edge_ref, sems, seq):
    after = {"seq": (seq + 1) % 32}
    before = {"seq": (seq + 31) % 32}
    (send_a, recv_a), (send_b, recv_b) = sems
    return [
        send(edge_ref.at[pl.ds(TOK, EDGE)], edge_ref.at[pl.ds(0, EDGE)], send_a, recv_a, after),
        send(
            edge_ref.at[pl.ds(EDGE, EDGE)],
            edge_ref.at[pl.ds(EDGE + TOK, EDGE)],
            send_b,
            recv_b,
            before,
        ),
    ]


def with_edges(edge_ref, seq):
    blank = jnp.zeros((EDGE, QW), jnp.bfloat16)
    head_rows = jnp.where(seq > 0, edge_ref[0:EDGE], blank)
    tail_rows = jnp.where(seq < 31, edge_ref[EDGE + TOK :], blank)
    return jnp.concatenate([head_rows, edge_ref[EDGE : EDGE + TOK], tail_rows], axis=0)


HALF, THIRD = QW // 2, QW // 3
WIDTHS = (THIRD, THIRD, THIRD, 2 * HEAD, HALF, HALF, HALF, HALF, HALF, HEAD)
TURNS = (1, 2, 3, 4, 0, 1, 2, 3, 4, 4)
PARTS = len(WIDTHS)
EARLY = (0, 1, 2, 3)
LATE = (4, 5, 6, 7, 8)
EMBED = 9
TAP_PAIRS = ((0, 1), (2, 3), (4, 4))


def chunk_owners(seq, turn, half):
    found = []
    for place in range(16 * half, 16 * half + 16):
        bits = [(place >> ((d - turn) % 5)) & 1 for d in range(5)]
        found.append(seq_peer(seq, bits))
    return found


def windows_of(padded, pair):
    turned = []
    for tap in sorted(set(pair)):
        window = padded[EDGE - 2 + tap : EDGE - 2 + tap + TOK].astype(jnp.float32).T
        turned.append(window.reshape(32, CH // 2, TOK))
    return jnp.concatenate([turned[0], turned[-1]], axis=1).astype(jnp.bfloat16)


def forward_kernel(
    slope_ref, shift_ref, words_ref, emb_w_ref, cot_ref, cw_hbm, qw_hbm, kvw_hbm, ow_hbm,
    att_ref, stat_ref, held_ref, q_ref, back_ref, hidden_ref, embedded_ref, normed_t_ref, cot_t_ref,
    win_ref, pwin_ref, edge_ref, act_land, turned_ref,
    cw_ref, qw_ref, kvw_ref, ow_ref, cot_full, kv_ref, normed_ref, acc_ref, top_ref, kpos_ref,
    load_sem, send_sem, recv_sem, hsend_sem, hrecv_sem, zsend_sem, zrecv_sem, msend_sem, mrecv_sem,
    asend_sem, arecv_sem,
):
    seq, tp = lax.axis_index("seq"), lax.axis_index("tp")
    loads = []
    for i, (far, near) in enumerate(
        ((ow_hbm, ow_ref), (cw_hbm, cw_ref), (qw_hbm, qw_ref), (kvw_hbm, kvw_ref))
    ):
        loads.append(pltpu.make_async_copy(far, near, load_sem.at[i]))
        loads[i].start()
    peers = [{"seq": one_move(seq, d)} for d in range(5)]
    side = {"tp": 1 - tp}
    enter(peers + [side, {"seq": (seq + 1) % 32}, {"seq": (seq + 31) % 32}])
    mine = pl.ds(pl.multiple_of(tp * QW, HEAD), QW)
    cot_copy = send(cot_ref, cot_full.at[:, mine], msend_sem.at[0], mrecv_sem.at[0], side)
    cot_copy.start()
    patches = unpack_bases(words_ref[...]).astype(jnp.bfloat16)
    embedded = dot_nn(patches, emb_w_ref[...]).astype(jnp.bfloat16)
    embedded_ref[...] = embedded
    embedded_wide = embedded.astype(jnp.float32)
    activated = gelu_value(embedded_wide * inverse_rms(embedded_wide))
    edge_ref[EDGE : EDGE + TOK] = activated.astype(jnp.bfloat16)
    edges = halo(
        edge_ref,
        ((msend_sem.at[1], mrecv_sem.at[1]), (msend_sem.at[2], mrecv_sem.at[2])),
        seq,
    )
    for copy in edges:
        copy.start()
    cot_full[:, mine] = cot_ref[...]
    cot_copy.wait()
    loads[0].wait()
    back_ref[...] = dot_nt(cot_full[...], ow_ref[...]).astype(jnp.bfloat16)
    for copy in edges:
        copy.wait()
    loads[1].wait()
    padded = with_edges(edge_ref, seq)
    edge_ref[...] = padded
    acts = []
    for d in range(5):
        copy = send(edge_ref, act_land.at[d], asend_sem.at[d], arecv_sem.at[d], peers[d])
        copy.start()
        acts.append(copy)
    hidden = embedded_ref[...].astype(jnp.float32)
    for tap in range(5):
        moved = dot_nn(padded, cw_ref[tap])
        hidden = hidden + moved[EDGE - 2 + tap : EDGE - 2 + tap + TOK]
    hidden_ref[:, mine] = hidden.astype(jnp.bfloat16)
    hidden_copy = send(
        hidden_ref.at[:, mine], hidden_ref.at[:, mine], msend_sem.at[3], mrecv_sem.at[3], side
    )
    hidden_copy.start()
    acc_ref[...] = jnp.zeros_like(acc_ref)
    top_ref[...] = jnp.full_like(top_ref, -1e30)
    hidden_copy.wait()
    loads[2].wait()
    loads[3].wait()
    hidden_wide = hidden_ref[...].astype(jnp.float32)
    normed_ref[...] = (hidden_wide * inverse_rms(hidden_wide)).astype(jnp.bfloat16)
    kv_ref[...] = dot_nn(normed_ref[...], kvw_ref[...]).astype(jnp.bfloat16)
    def own_half(half):
        rows = pl.ds(half * KV_ROWS, KV_ROWS)
        copies = []
        for k in (3, 2, 1, 0):
            for part in range(KV_PARTS):
                copy = send(
                    held_ref.at[0, part, rows],
                    held_ref.at[2**k, part, rows],
                    hsend_sem.at[half, k, part],
                    hrecv_sem.at[half, k, part],
                    peers[(part + k) % 4],
                )
                copy.start()
                copies.append((2**k, copy))
        return copies

    arrivals = {place: [] for place in range(1, 16)}

    def pass_on(place):
        for k in range(place.bit_length(), 4):
            for part in range(KV_PARTS):
                copy = send(
                    held_ref.at[place, part],
                    held_ref.at[2**k + place, part],
                    send_sem.at[2**k + place, part],
                    recv_sem.at[2**k + place, part],
                    peers[(part + k) % 4],
                )
                copy.start()
                arrivals[2**k + place].append(copy)

    def receive(*places_now):
        for place in places_now:
            for copy in arrivals[place]:
                copy.wait()
            pass_on(place)

    zcopies = []
    for part in range(KV_PARTS):
        rows = pl.ds(part * KV_ROWS, KV_ROWS)
        copy = send(
            kv_ref.at[rows],
            held_ref.at[0, part, pl.ds(KV_ROWS, KV_ROWS)],
            zsend_sem.at[part],
            zrecv_sem.at[part],
            peers[4],
        )
        copy.start()
        zcopies.append(copy)
    for part in range(KV_PARTS):
        held_ref[0, part, 0:KV_ROWS] = kv_ref[part * KV_ROWS : (part + 1) * KV_ROWS]
    first_half = own_half(0)
    q_ref[...] = dot_nn(normed_ref[...], qw_ref[...]).astype(jnp.bfloat16)
    column = lax.broadcasted_iota(jnp.int32, (TOK, 1), 0)
    qpos = (column + (seq * TOK + shift_ref[0])).astype(jnp.float32)
    lane = lax.broadcasted_iota(jnp.int32, (1, 2 * TOK), 1)
    ys, xs, zs = pick(seq // 8), pick((seq // 2) % 4), [seq % 2, 1 - seq % 2]
    for place in range(16):
        kpos = lane % KV_ROWS
        for part in range(KV_PARTS):
            m = place_moves(part, place)
            for z in range(2):
                source = (ys[m[2] ^ 3 * m[3]] * 4 + xs[m[0] ^ 3 * m[1]]) * 2 + zs[z]
                here = lane // KV_ROWS == 2 * part + z
                kpos = kpos + jnp.where(here, source * TOK + part * KV_ROWS, 0)
        kpos_ref[place] = kpos.astype(jnp.float32)

    def absorb(pair, kpos):
        keys = pair[:, :HEAD]
        values = jnp.concatenate([pair[:, HEAD:], jnp.ones_like(keys)], axis=1)
        distance = jnp.abs(qpos - kpos)
        for head in range(MEMBERS):
            scores = dot_nt(q_ref[:, head * HEAD : (head + 1) * HEAD], keys) * SCORE_SCALE
            scores = scores - distance * (slope_ref[head] * BIAS_SCALE)
            old = top_ref[head]
            new = jnp.maximum(old, jnp.max(scores, axis=1, keepdims=True))
            fading = jnp.exp2(old - new)
            weights = jnp.exp2(scores - new[:, :1]).astype(jnp.bfloat16)
            acc_ref[head] = acc_ref[head] * jnp.concatenate([fading, fading], axis=1) + dot_nn(
                weights, values
            )
            top_ref[head] = new

    def places(first, count):
        pair = held_ref[pl.ds(first, count)].reshape(count * 2 * TOK, 2 * HEAD)
        if count == 1:
            kpos = kpos_ref[first]
        else:
            kpos = jnp.concatenate([kpos_ref[first + i] for i in range(count)], axis=1)
        absorb(pair, kpos)

    def turned(ref, target, first, count):
        columns = slice(first * 2 * CH * 4, (first + count) * 2 * CH * 4)
        block = ref[:, columns].astype(jnp.float32).T.astype(jnp.bfloat16)
        target[8 * first : 8 * (first + count)] = block.reshape(8 * count, CH, TOK)

    def own_windows(i):
        win_ref[i] = windows_of(edge_ref, TAP_PAIRS[i])

    def peer_windows(i):
        turn = TURNS[LATE[i]]
        turned_ref[...] = windows_of(act_land.at[(turn + 4) % 5], TAP_PAIRS[i // 2])
        for j, owner in enumerate(chunk_owners(seq, turn, 0)):
            pwin_ref[i, j] = turned_ref[owner]

    for copy in zcopies:
        copy.wait()
    for place, copy in first_half + own_half(1):
        arrivals[place].append(copy)
    places(0, 1)
    own_windows(0)
    receive(1, 2, 4)
    own_windows(1)
    places(1, 2)
    receive(3, 5, 6)
    own_windows(2)
    places(3, 2)
    for copy in acts:
        copy.wait()
    receive(7)
    peer_windows(0)
    peer_windows(1)
    places(5, 3)
    peer_windows(2)
    peer_windows(3)
    peer_windows(4)
    receive(8, 9, 10, 11)
    places(8, 4)
    turned(cot_full, cot_t_ref, 0, 4)
    turned(normed_ref, normed_t_ref, 0, 4)
    receive(12, 13, 14, 15)
    places(12, 4)
    lane = lax.broadcasted_iota(jnp.int32, (TOK, HEAD), 1)
    stats = jnp.zeros((TOK, HEAD), jnp.float32)
    for head in range(MEMBERS):
        totals = acc_ref[head, :, HEAD:]
        mixed = (acc_ref[head, :, :HEAD] / totals).astype(jnp.bfloat16)
        att_ref[:, head * HEAD : (head + 1) * HEAD] = mixed
        back = back_ref[:, head * HEAD : (head + 1) * HEAD].astype(jnp.float32)
        delta = jnp.sum(back * mixed.astype(jnp.float32), axis=1, keepdims=True)
        stats = jnp.where(lane == head, top_ref[head] + jnp.log2(totals), stats)
        stats = jnp.where(lane == 8 + head, delta, stats)
    turned_stats = stats.T
    for duo in range(MEMBERS // 2):
        for i in range(2):
            row = 2 * duo + i
            stat_ref[duo, :, i * TOK : (i + 1) * TOK] = turned_stats[row : row + 1]
            row = 2 * duo + i + 8
            stat_ref[3 + duo, :, i * TOK : (i + 1) * TOK] = turned_stats[row : row + 1]


def forward_attention(*operands):
    vmem = pl.BlockSpec(memory_space=pltpu.VMEM)
    f32, bf16 = jnp.float32, jnp.bfloat16
    return pl.pallas_call(
        forward_kernel,
        out_shape=(
            jax.ShapeDtypeStruct((TOK, QW), bf16),
            jax.ShapeDtypeStruct((6, 1, 2 * TOK), f32),
            jax.ShapeDtypeStruct((16, KV_PARTS, 2 * KV_ROWS, 2 * HEAD), bf16),
            jax.ShapeDtypeStruct((TOK, QW), bf16),
            jax.ShapeDtypeStruct((TOK, QW), bf16),
            jax.ShapeDtypeStruct((TOK, 2 * QW), bf16),
            jax.ShapeDtypeStruct((TOK, QW), bf16),
            jax.ShapeDtypeStruct((32, CH, TOK), bf16),
            jax.ShapeDtypeStruct((32, CH, TOK), bf16),
            jax.ShapeDtypeStruct((3, 32, CH, TOK), bf16),
            jax.ShapeDtypeStruct((5, 16, CH, TOK), bf16),
        ),
        in_specs=[pl.BlockSpec(memory_space=pltpu.SMEM)] * 2
        + [vmem] * 3
        + [pl.BlockSpec(memory_space=pl.ANY)] * 4,
        out_specs=(vmem,) * 11,
        scratch_shapes=[
            pltpu.VMEM((TOK + 2 * EDGE, QW), bf16),
            pltpu.VMEM((5, TOK + 2 * EDGE, QW), bf16),
            pltpu.VMEM((32, CH, TOK), bf16),
            pltpu.VMEM((5, QW, QW), bf16),
            pltpu.VMEM((2 * QW, QW), bf16),
            pltpu.VMEM((2 * QW, 2 * HEAD), bf16),
            pltpu.VMEM((QW, 2 * QW), bf16),
            pltpu.VMEM((TOK, 2 * QW), bf16),
            pltpu.VMEM((TOK, 2 * HEAD), bf16),
            pltpu.VMEM((TOK, 2 * QW), bf16),
            pltpu.VMEM((MEMBERS, TOK, 2 * HEAD), f32),
            pltpu.VMEM((MEMBERS, TOK, HEAD), f32),
            pltpu.VMEM((16, 1, 2 * TOK), f32),
            pltpu.SemaphoreType.DMA((4,)),
            pltpu.SemaphoreType.DMA((16, KV_PARTS)),
            pltpu.SemaphoreType.DMA((16, KV_PARTS)),
            pltpu.SemaphoreType.DMA((2, 4, KV_PARTS)),
            pltpu.SemaphoreType.DMA((2, 4, KV_PARTS)),
            pltpu.SemaphoreType.DMA((KV_PARTS,)),
            pltpu.SemaphoreType.DMA((KV_PARTS,)),
            pltpu.SemaphoreType.DMA((4,)),
            pltpu.SemaphoreType.DMA((4,)),
            pltpu.SemaphoreType.DMA((5,)),
            pltpu.SemaphoreType.DMA((5,)),
        ],
        compiler_params=pltpu.CompilerParams(
            collective_id=0, has_side_effects=True, vmem_limit_bytes=VMEM_LIMIT
        ),
    )(*operands)


class Halving:
    def __init__(self, turns, sums, lands, send_sem, recv_sem, seq):
        self.turns, self.sums, self.lands = turns, sums, lands
        self.send_sem, self.recv_sem = send_sem, recv_sem
        self.peers = [{"seq": one_move(seq, d)} for d in range(5)]
        self.seq, self.flights = seq, {}

    def owners(self, part, half):
        return chunk_owners(self.seq, self.turns[part], half)

    def start(self, part, k):
        copies = []
        if k > 0:
            spans = ((2 ** (k - 1), 2 ** (k - 1)), (0, 2 ** (k - 1)))
        else:
            spans = ((0, 1),)
        for piece, (low, count) in enumerate(spans):
            copy = send(
                self.sums[part].at[pl.ds(2**k + low, count)],
                self.lands[part].at[pl.ds(2**k + low, count)],
                self.send_sem.at[part, k, piece],
                self.recv_sem.at[part, k, piece],
                self.peers[(self.turns[part] + k) % 5],
            )
            copy.start()
            copies.append((copy, low, count))
        return copies

    def settle(self, part, k, item):
        copy, low, count = item
        copy.wait()
        bunch = min(count, 4)
        total, landed = self.sums[part], self.lands[part]

        def add(i, carry):
            at = pl.ds(low + i * bunch, bunch)
            total[at] = total[at] + landed[pl.ds(2**k + low + i * bunch, bunch)]
            return carry

        lax.fori_loop(0, count // bunch, add, 0)

    def launch(self, part, k=4):
        self.flights[part] = self.start(part, k)

    def advance(self, parts, k):
        following = {}
        for part in parts:
            self.settle(part, k, self.flights[part][0])
            following[part] = self.start(part, k - 1)
        for part in parts:
            self.settle(part, k, self.flights[part][1])
        self.flights.update(following)


def chunk_rows(ref, owners, count):
    return jnp.concatenate([ref[owner, 0:count] for owner in owners], axis=0)


OUT_PARTS = 3
OUT_WIDTH = QW // OUT_PARTS


def backward_kernel(
    slope_ref, shift_ref, q_ref, back_ref, held_ref, stat_ref, cot_t_ref, att_ref,
    dq_ref, dkv_ref, out_ref,
    qs_ref, bs_ref, dq_acc, part_ref, land3, land2, land1, land0, landz,
    sums0, sums1, sums2, lands0, lands1, lands2, dp_lands,
    send_sem, recv_sem, zsend_sem, zrecv_sem, osend_sem, orecv_sem, fsend_sem, frecv_sem,
    *, factor,
):
    seq, dp = lax.axis_index("seq"), lax.axis_index("dp")
    peers = [{"seq": one_move(seq, d)} for d in range(5)]
    over = {"dp": 1 - dp}
    enter(peers + [over])
    outs = Halving(
        (2, 0, 4), (sums0, sums1, sums2), (lands0, lands1, lands2), osend_sem, orecv_sem, seq
    )
    out_parts = range(OUT_PARTS)

    def fill(part, half):
        columns = slice(part * OUT_WIDTH, (part + 1) * OUT_WIDTH)
        grads = dot_nn(chunk_rows(cot_t_ref, outs.owners(part, half), CH), att_ref[:, columns])
        outs.sums[part][16 * half : 16 * half + 16] = grads.astype(jnp.bfloat16).reshape(
            16, CH, OUT_WIDTH
        )

    for part in out_parts:
        fill(part, 1)
        outs.launch(part)
    lands = [land0, land1, land2, land3]
    for head in range(MEMBERS):
        rows = slice(head * TOK, (head + 1) * TOK)
        qs_ref[rows] = q_ref[:, head * HEAD : (head + 1) * HEAD]
        bs_ref[rows] = back_ref[:, head * HEAD : (head + 1) * HEAD]
    dq_acc[...] = jnp.zeros_like(dq_acc)
    lane = lax.broadcasted_iota(jnp.int32, (1, 2 * TOK), 1)
    qpos = (lane % TOK + (seq * TOK + shift_ref[0])).astype(jnp.float32)
    slopes = [
        jnp.where(lane < TOK, slope_ref[2 * duo], slope_ref[2 * duo + 1]) * BIAS_SCALE
        for duo in range(MEMBERS // 2)
    ]
    row = lax.broadcasted_iota(jnp.int32, (KV_ROWS, 1), 0)

    def work(first, count):
        size = count * 2 * TOK
        pair = held_ref[pl.ds(first, count)].reshape(size, 2 * HEAD)
        keys, values = pair[:, :HEAD], pair[:, HEAD:]
        kpos = []
        for i in range(count):
            for part in range(KV_PARTS):
                for z in range(2):
                    source = seq_peer(seq, place_moves(part, first + i) + [z])
                    kpos.append(row + (source * TOK + part * KV_ROWS))
        distance = jnp.abs(qpos - jnp.concatenate(kpos, axis=0).astype(jnp.float32))
        all_probs, all_grads = [], []
        for duo in range(MEMBERS // 2):
            rows = slice(duo * 2 * TOK, (duo + 1) * 2 * TOK)
            scores = dot_nt(keys, qs_ref[rows]) * SCORE_SCALE - distance * slopes[duo]
            probs = jnp.exp2(scores - stat_ref[duo])
            back_probs = dot_nt(values, bs_ref[rows])
            all_grads.append((probs * (back_probs - stat_ref[3 + duo])).astype(jnp.bfloat16))
            all_probs.append(probs.astype(jnp.bfloat16))
        grad_scores = jnp.concatenate(all_grads, axis=1)
        value_grad = dot_nn(jnp.concatenate(all_probs, axis=1), bs_ref[...])
        key_grad = dot_nn(grad_scores, qs_ref[...])
        dq_acc[...] += dot_tn(grad_scores, keys)
        both = jnp.concatenate([key_grad * (1.0 / math.sqrt(HEAD)), value_grad], axis=1)
        part_ref[pl.ds(first, count)] = both.astype(jnp.bfloat16).reshape(
            count, KV_PARTS, 2 * KV_ROWS, 2 * HEAD
        )

    def piece_copies(number, k, first, count):
        return [
            send(
                part_ref.at[pl.ds(first, count), part],
                lands[k].at[pl.ds(first - 2**k, count), part],
                send_sem.at[number, part],
                recv_sem.at[number, part],
                peers[(part + k) % 4],
            )
            for part in range(KV_PARTS)
        ]

    def start_piece(*piece):
        copies = piece_copies(*piece)
        for copy in copies:
            copy.start()
        return copies

    def take_in(place, stages, pieces):
        for copies in pieces:
            for copy in copies:
                copy.wait()
        total = part_ref[place].astype(jnp.float32)
        for k in stages:
            total = total + lands[k][place].astype(jnp.float32)
        part_ref[place] = total.astype(jnp.bfloat16)

    def outer_places(i, carry):
        first = 14 - 2 * i
        work(first, 2)
        for copy in piece_copies(i, 3, first, 2):
            copy.start()
        return carry

    def inner_places(i, carry):
        work(2 * i, 2)
        return carry

    for part in out_parts:
        fill(part, 0)
    lax.fori_loop(0, 4, outer_places, 0)
    third = [piece_copies(i, 3, 14 - 2 * i, 2) for i in range(4)]
    outs.advance(out_parts, 4)
    lax.fori_loop(3, 4, inner_places, 0)
    take_in(6, (3,), [third[0]])
    take_in(7, (3,), [])
    second = [start_piece(4, 2, 6, 2)]
    outs.advance(out_parts, 3)
    lax.fori_loop(2, 3, inner_places, 0)
    take_in(4, (3,), [third[1]])
    take_in(5, (3,), [])
    second.append(start_piece(5, 2, 4, 2))
    outs.advance(out_parts, 2)
    lax.fori_loop(1, 2, inner_places, 0)
    take_in(2, (2, 3), [third[2], second[0]])
    take_in(3, (2, 3), [])
    first = start_piece(6, 1, 2, 2)
    outs.advance(out_parts, 1)
    lax.fori_loop(0, 1, inner_places, 0)
    take_in(1, (1, 2, 3), [third[3], second[1], first])
    last = start_piece(7, 0, 1, 1)
    finals = []
    for part in out_parts:
        outs.settle(part, 0, outs.flights[part][0])
        copy = send(
            outs.sums[part].at[0], dp_lands.at[part], fsend_sem.at[part], frecv_sem.at[part], over
        )
        copy.start()
        finals.append(copy)
    take_in(0, (0, 1, 2, 3), [last])
    zcopies = []
    for part in range(KV_PARTS):
        copy = send(
            part_ref.at[0, part, pl.ds(KV_ROWS, KV_ROWS)],
            landz.at[part],
            zsend_sem.at[part],
            zrecv_sem.at[part],
            peers[4],
        )
        copy.start()
        zcopies.append(copy)
    for head in range(MEMBERS):
        grad = dq_acc[head * TOK : (head + 1) * TOK] * (1.0 / math.sqrt(HEAD))
        dq_ref[:, head * HEAD : (head + 1) * HEAD] = grad.astype(jnp.bfloat16)
    for part in out_parts:
        finals[part].wait()
        total = outs.sums[part][0].astype(jnp.float32) + dp_lands[part].astype(jnp.float32)
        out_ref[:, part * OUT_WIDTH : (part + 1) * OUT_WIDTH] = total * factor
    for part in range(KV_PARTS):
        zcopies[part].wait()
        dkv_ref[part * KV_ROWS : (part + 1) * KV_ROWS] = part_ref[0, part, 0:KV_ROWS] + landz[part]


def backward_attention(factor, *operands):
    vmem = pl.BlockSpec(memory_space=pltpu.VMEM)
    f32, bf16 = jnp.float32, jnp.bfloat16
    block = (KV_PARTS, 2 * KV_ROWS, 2 * HEAD)
    return pl.pallas_call(
        functools.partial(backward_kernel, factor=factor),
        out_shape=(
            jax.ShapeDtypeStruct((TOK, QW), bf16),
            jax.ShapeDtypeStruct((TOK, 2 * HEAD), bf16),
            jax.ShapeDtypeStruct((CH, QW), f32),
        ),
        in_specs=[pl.BlockSpec(memory_space=pltpu.SMEM)] * 2 + [vmem] * 6,
        out_specs=(vmem,) * 3,
        scratch_shapes=[
            pltpu.VMEM((MEMBERS * TOK, HEAD), bf16),
            pltpu.VMEM((MEMBERS * TOK, HEAD), bf16),
            pltpu.VMEM((MEMBERS * TOK, HEAD), f32),
            pltpu.VMEM((16,) + block, bf16),
            pltpu.VMEM((8,) + block, bf16),
            pltpu.VMEM((4,) + block, bf16),
            pltpu.VMEM((2,) + block, bf16),
            pltpu.VMEM((1,) + block, bf16),
            pltpu.VMEM((KV_PARTS, KV_ROWS, 2 * HEAD), bf16),
        ]
        + [pltpu.VMEM((32, CH, OUT_WIDTH), bf16)] * 6
        + [
            pltpu.VMEM((OUT_PARTS, CH, OUT_WIDTH), bf16),
            pltpu.SemaphoreType.DMA((8, KV_PARTS)),
            pltpu.SemaphoreType.DMA((8, KV_PARTS)),
            pltpu.SemaphoreType.DMA((KV_PARTS,)),
            pltpu.SemaphoreType.DMA((KV_PARTS,)),
            pltpu.SemaphoreType.DMA((OUT_PARTS, 5, 2)),
            pltpu.SemaphoreType.DMA((OUT_PARTS, 5, 2)),
            pltpu.SemaphoreType.DMA((OUT_PARTS,)),
            pltpu.SemaphoreType.DMA((OUT_PARTS,)),
        ],
        compiler_params=pltpu.CompilerParams(
            collective_id=1, has_side_effects=True, vmem_limit_bytes=VMEM_LIMIT
        ),
    )(*operands)


def weights_kernel(
    normed_ref, words_ref,
    dq_ref, att_ref, pair_ref, hidden_ref, embedded_ref, cotangent_ref,
    win_hbm, pwin_hbm, cw_hbm, qw_hbm, kvw_hbm, ow_hbm,
    result_out, query_out, pair_out, conv_out, embed_out,
    *scratch, factor,
):
    sums, lands = scratch[:PARTS], scratch[PARTS : 2 * PARTS]
    dp_lands = scratch[2 * PARTS : 3 * PARTS]
    (
        cw_ref, qw_ref, kvw_ref, ow_ref, win_ref, pwin_ref, conv_land, patch_ref, out_own, out_side,
        wide_own, wide_side, edge_ref, conv_side, active_own, active_side, emb_ref,
        land_tp, land_diag, load_sem, send_sem, recv_sem, fsend_sem, frecv_sem, csend_sem, crecv_sem,
    ) = scratch[3 * PARTS :]
    seq, dp, tp = lax.axis_index("seq"), lax.axis_index("dp"), lax.axis_index("tp")
    loads = []
    for i, (far, near) in enumerate(
        (
            (qw_hbm, qw_ref), (kvw_hbm, kvw_ref), (cw_hbm, cw_ref), (win_hbm, win_ref),
            (pwin_hbm, pwin_ref), (ow_hbm, ow_ref),
        )
    ):
        loads.append(pltpu.make_async_copy(far, near, load_sem.at[i]))
        loads[i].start()
    peers = [{"seq": one_move(seq, d)} for d in range(5)]
    over = {"dp": 1 - dp}
    side = {"tp": 1 - tp}
    diagonal = {"dp": 1 - dp, "tp": 1 - tp}
    around = [{"seq": (seq + 1) % 32}, {"seq": (seq + 31) % 32}]
    enter(peers + [over, side, diagonal] + around)
    left_rows = lax.broadcasted_iota(jnp.int32, (16 * CH, HALF), 0) % CH < CH // 2

    run = Halving(TURNS, sums, lands, send_sem, recv_sem, seq)
    conv = slice(EDGE, EDGE + TOK)

    def fill(part, half):
        owners = run.owners(part, half)
        if part < 3:
            columns = slice(part * THIRD, (part + 1) * THIRD)
            grads = dot_nn(chunk_rows(normed_ref, owners, CH), dq_ref[:, columns])
        elif part == 3:
            grads = dot_nn(chunk_rows(normed_ref, owners, CH), pair_ref[...])
        else:
            columns = pl.ds(pl.multiple_of(tp * HALF, HEAD), HALF)
            emb = dot_nn(chunk_rows(patch_ref, owners, 16), emb_ref[:, columns])
            grads = jnp.concatenate(
                [
                    emb[16 * j : 16 * j + 16, HEAD * c : HEAD * c + HEAD]
                    for j in range(16)
                    for c in range(3)
                ],
                axis=0,
            )
        sums[part][16 * half : 16 * half + 16] = grads.astype(jnp.bfloat16).reshape(
            16, CH, WIDTHS[part]
        )

    def conv_columns(part):
        if part == LATE[4]:
            return slice(0, QW)
        return slice((part - LATE[0]) % 2 * HALF, ((part - LATE[0]) % 2 + 1) * HALF)

    def conv_exchange(part):
        i, columns = part - LATE[0], conv_columns(part)
        width = columns.stop - columns.start
        copy = send(
            edge_ref.at[pl.ds(EDGE, TOK), pl.ds(columns.start, width)],
            conv_land.at[i, :, pl.ds(0, width)],
            csend_sem.at[i],
            crecv_sem.at[i],
            run.peers[(TURNS[part] + 4) % 5],
        )
        copy.start()
        return copy

    def fill_conv(part):
        i, columns = part - LATE[0], conv_columns(part)
        width = columns.stop - columns.start
        own_rows = chunk_rows(win_ref.at[i // 2], run.owners(part, 0), CH)
        peer_rows = pwin_ref[i].reshape(16 * CH, TOK)
        grads = dot_nn(own_rows, edge_ref[conv, columns]) + dot_nn(
            peer_rows, conv_land[i, :, :width]
        )
        if part == LATE[4]:
            grads = jnp.where(left_rows, grads[:, :HALF], grads[:, HALF:])
        sums[part][...] = grads.astype(jnp.bfloat16).reshape(16, CH, HALF)

    finals = {}

    def finish(parts):
        for part in parts:
            run.settle(part, 0, run.flights[part][0])
            copy = send(
                sums[part].at[0], dp_lands[part], fsend_sem.at[part], frecv_sem.at[part], over
            )
            copy.start()
            finals[part] = copy

    def total(part):
        finals[part].wait()
        return (sums[part][0].astype(jnp.float32) + dp_lands[part][...].astype(jnp.float32)) * factor

    for part in EARLY:
        fill(part, 1)
        run.launch(part)
    loads[0].wait()
    loads[1].wait()
    partial = dot_nt(dq_ref[...], qw_ref[...]) + dot_nt(pair_ref[...], kvw_ref[...])
    wide_own[...] = partial.astype(jnp.bfloat16)
    wide_copy = send(wide_own, wide_side, fsend_sem.at[PARTS + 0], frecv_sem.at[PARTS + 0], side)
    wide_copy.start()
    for part in EARLY:
        fill(part, 0)
    patches = unpack_bases(words_ref[...]).T
    patch_ref[...] = patches.reshape(32, 16, TOK).astype(jnp.bfloat16)
    hidden = hidden_ref[...].astype(jnp.float32)
    scale = inverse_rms(hidden)
    wide_copy.wait()
    back_normed = wide_own[...].astype(jnp.float32) + wide_side[...].astype(jnp.float32)
    mean = jnp.mean(back_normed * (hidden * scale), axis=-1, keepdims=True)
    mine = pl.ds(pl.multiple_of(tp * QW, HEAD), QW)
    own = wide_own[:, mine].astype(jnp.float32) + wide_side[:, mine].astype(jnp.float32)
    normed = hidden_ref[:, mine].astype(jnp.float32) * scale
    back_hidden = cotangent_ref[...].astype(jnp.float32) + scale * (own - normed * mean)
    edge_ref[EDGE : EDGE + TOK] = back_hidden.astype(jnp.bfloat16)
    edge_copies = halo(
        edge_ref,
        ((fsend_sem.at[PARTS + 1], frecv_sem.at[PARTS + 1]), (fsend_sem.at[PARTS + 2], frecv_sem.at[PARTS + 2])),
        seq,
    )
    for copy in edge_copies:
        copy.start()
    conv_copy = send(
        edge_ref.at[pl.ds(EDGE, TOK)], conv_side, fsend_sem.at[PARTS + 3], frecv_sem.at[PARTS + 3], side
    )
    conv_copy.start()
    exchanges = {part: conv_exchange(part) for part in LATE}
    for i in range(2, 5):
        loads[i].wait()
    for copy in edge_copies:
        copy.wait()
    padded = with_edges(edge_ref, seq)
    active = jnp.zeros((TOK, QW), jnp.float32)
    for tap in range(5):
        moved = dot_nt(padded, cw_ref[tap])
        active = active + moved[EDGE + 2 - tap : EDGE + 2 - tap + TOK]
    active_own[...] = active.astype(jnp.bfloat16)
    active_copy = send(active_own, active_side, fsend_sem.at[PARTS + 4], frecv_sem.at[PARTS + 4], side)
    active_copy.start()
    loads[5].wait()
    out_own[...] = dot_nn(att_ref[...], ow_ref[...]).astype(jnp.bfloat16)
    theirs = pl.ds(pl.multiple_of((1 - tp) * QW, HEAD), QW)
    out_copy = send(out_own.at[:, theirs], out_side, fsend_sem.at[PARTS + 7], frecv_sem.at[PARTS + 7], side)
    out_copy.start()
    for part in LATE:
        exchanges[part].wait()
        fill_conv(part)
        run.launch(part, 3)
    embedded = embedded_ref[...].astype(jnp.float32)
    scale_in = inverse_rms(embedded)
    normed_in = embedded * scale_in
    slope = gelu_slope(normed_in)
    conv_copy.wait()
    residual = edge_ref[EDGE : EDGE + TOK].astype(jnp.float32) + conv_side[...].astype(jnp.float32)
    active_copy.wait()
    back_in = (active_own[...].astype(jnp.float32) + active_side[...].astype(jnp.float32)) * slope
    mean_in = jnp.mean(back_in * normed_in, axis=-1, keepdims=True)
    emb_ref[...] = (residual + scale_in * (back_in - normed_in * mean_in)).astype(jnp.bfloat16)
    fill(EMBED, 1)
    run.launch(EMBED)
    fill(EMBED, 0)
    run.advance(EARLY, 4)
    out_copy.wait()
    projected = out_own[:, mine].astype(jnp.float32) + out_side[...].astype(jnp.float32)
    result_out[...] = (hidden_ref[:, mine].astype(jnp.float32) + projected).astype(jnp.bfloat16)
    run.advance(EARLY, 3)
    run.advance((EMBED,), 4)
    run.advance(LATE, 3)
    run.advance(EARLY, 2)
    run.advance((EMBED,), 3)
    run.advance(LATE, 2)
    run.advance(EARLY, 1)
    run.advance((EMBED,), 2)
    finish(EARLY)
    run.advance(LATE, 1)
    run.advance((EMBED,), 1)
    finish(LATE + (EMBED,))
    sidecopy = send(sums[EMBED].at[0], land_tp, fsend_sem.at[PARTS + 5], frecv_sem.at[PARTS + 5], side)
    sidecopy.start()
    diagcopy = send(sums[EMBED].at[0], land_diag, fsend_sem.at[PARTS + 6], frecv_sem.at[PARTS + 6], diagonal)
    diagcopy.start()
    for third in range(3):
        query_out[:, third * THIRD : (third + 1) * THIRD] = total(third)
    pair_out[...] = total(3)
    rows = CH // 2
    for part in range(4):
        tap, columns = part // 2 * 2, slice(part % 2 * HALF, (part % 2 + 1) * HALF)
        block = total(LATE[part])
        conv_out[tap, :, columns] = block[:rows]
        conv_out[tap + 1, :, columns] = block[rows:]
    block = total(LATE[4])
    conv_out[4, :, :HALF] = block[:rows]
    conv_out[4, :, HALF:] = block[rows:]

    def embed_store(block, core):
        wide = jnp.concatenate([block[:16], block[16:32], block[32:]], axis=1)
        embed_out[:, pl.ds(pl.multiple_of(core * HALF, HEAD), HALF)] = wide

    embed_store(total(EMBED), tp)
    sidecopy.wait()
    diagcopy.wait()
    other = land_tp[...].astype(jnp.float32) + land_diag[...].astype(jnp.float32)
    embed_store(other * factor, 1 - tp)


def weight_gradients(factor, *operands):
    vmem = pl.BlockSpec(memory_space=pltpu.VMEM)
    f32, bf16 = jnp.float32, jnp.bfloat16
    return pl.pallas_call(
        functools.partial(weights_kernel, factor=factor),
        out_shape=(
            jax.ShapeDtypeStruct((TOK, QW), bf16),
            jax.ShapeDtypeStruct((CH, QW), f32),
            jax.ShapeDtypeStruct((CH, 2 * HEAD), f32),
            jax.ShapeDtypeStruct((5, CH // 2, QW), f32),
            jax.ShapeDtypeStruct((16, QW), f32),
        ),
        in_specs=[vmem] * 8 + [pl.BlockSpec(memory_space=pl.ANY)] * 6,
        out_specs=(vmem,) * 5,
        scratch_shapes=[
            pltpu.VMEM((16 if part in LATE else 32, CH, w), bf16) for part, w in enumerate(WIDTHS)
        ]
        * 2
        + [pltpu.VMEM((CH, w), bf16) for w in WIDTHS]
        + [
            pltpu.VMEM((5, QW, QW), bf16),
            pltpu.VMEM((2 * QW, QW), bf16),
            pltpu.VMEM((2 * QW, 2 * HEAD), bf16),
            pltpu.VMEM((QW, 2 * QW), bf16),
            pltpu.VMEM((3, 32, CH, TOK), bf16),
            pltpu.VMEM((5, 16, CH, TOK), bf16),
            pltpu.VMEM((5, TOK, QW), bf16),
            pltpu.VMEM((32, 16, TOK), bf16),
            pltpu.VMEM((TOK, 2 * QW), bf16),
            pltpu.VMEM((TOK, QW), bf16),
            pltpu.VMEM((TOK, 2 * QW), bf16),
            pltpu.VMEM((TOK, 2 * QW), bf16),
            pltpu.VMEM((TOK + 2 * EDGE, QW), bf16),
            pltpu.VMEM((TOK, QW), bf16),
            pltpu.VMEM((TOK, QW), bf16),
            pltpu.VMEM((TOK, QW), bf16),
            pltpu.VMEM((TOK, QW), bf16),
            pltpu.VMEM((CH, HEAD), bf16),
            pltpu.VMEM((CH, HEAD), bf16),
            pltpu.SemaphoreType.DMA((6,)),
            pltpu.SemaphoreType.DMA((PARTS, 5, 2)),
            pltpu.SemaphoreType.DMA((PARTS, 5, 2)),
            pltpu.SemaphoreType.DMA((PARTS + 8,)),
            pltpu.SemaphoreType.DMA((PARTS + 8,)),
            pltpu.SemaphoreType.DMA((5,)),
            pltpu.SemaphoreType.DMA((5,)),
        ],
        compiler_params=pltpu.CompilerParams(
            collective_id=2, has_side_effects=True, vmem_limit_bytes=VMEM_LIMIT
        ),
    )(*operands)


def last_kernel(*refs):
    result, query, output, pair, conv, embed = refs[:6]
    result_out, query_out, output_out, pair_out, conv_out, embed_out = refs[6:]
    result_out[...] = result[...]
    query_out[...] = query[...]
    output_out[...] = output[...]
    pair_out[:, 0, :] = pair[...]
    conv_out[...] = conv[...]
    embed_out[...] = embed[...]


def write_outputs(*operands):
    vmem = pl.BlockSpec(memory_space=pltpu.VMEM)
    shapes = [jax.ShapeDtypeStruct(o.shape, o.dtype) for o in operands]
    shapes[3] = jax.ShapeDtypeStruct((CH, 1, 2 * HEAD), jnp.float32)
    return pl.pallas_call(
        last_kernel,
        out_shape=tuple(shapes),
        in_specs=[vmem] * 6,
        out_specs=(vmem,) * 6,
    )(*operands)


def per_device(
    bases,
    shifts,
    embed_weight,
    conv_weight,
    query_weight,
    keyvalue_weight,
    output_weight,
    slopes,
    cotangent,
):
    tokens = cotangent.shape[1]
    words = bases.reshape(tokens, -1)
    pair_weight = keyvalue_weight.reshape(2 * QW, 2 * HEAD)
    cotangent_local = cotangent[0]
    factor = (lax.axis_size("dp") * lax.axis_size("seq") * tokens) ** (-0.5)
    (
        attended, stats, held, queries, back_attended, hidden, embedded, normed_t, cot_t, win, peer_win
    ) = forward_attention(
        slopes,
        shifts,
        words,
        embed_weight,
        cotangent_local,
        conv_weight,
        query_weight,
        pair_weight,
        output_weight,
    )
    back_query, back_pair, grad_output = backward_attention(
        factor, slopes, shifts, queries, back_attended, held, stats, cot_t, attended
    )
    result, grad_query, grad_pair, grad_conv, grad_embed = weight_gradients(
        factor,
        normed_t,
        words,
        back_query,
        attended,
        back_pair,
        hidden,
        embedded,
        cotangent_local,
        win,
        peer_win,
        conv_weight,
        query_weight,
        pair_weight,
        output_weight,
    )
    result, grad_query, grad_output, grad_pair, grad_conv, grad_embed = write_outputs(
        result, grad_query, grad_output, grad_pair, grad_conv, grad_embed
    )
    return (result[None], grad_embed, grad_conv, grad_query, grad_pair, grad_output.T)


def solution(mesh):
    placed = (
        P("dp", "seq"),
        P("dp"),
        P(),
        P(None, None, "tp"),
        P(None, "tp"),
        P(None, "tp", None),
        P("tp", None),
        P("tp"),
        P("dp", "seq", "tp"),
    )
    return jax.shard_map(
        per_device,
        mesh=mesh,
        in_specs=placed,
        out_specs=(
            P("dp", "seq", "tp"),
            P("seq", None),
            P(None, "seq", "tp"),
            P("seq", "tp"),
            P("seq", "tp", None),
            P("tp", "seq"),
        ),
        check_vma=False,
    )
```

```python
import functools
import math

import jax
import jax.numpy as jnp
from jax import lax
from jax.experimental import pallas as pl
from jax.experimental.pallas import tpu as pltpu
from jax.sharding import PartitionSpec as P

ROOT_TWO_PI = math.sqrt(2.0 / math.pi)
CUBIC = 0.044715
EPSILON = 1e-06
DISTANCE_SCALE = 128.0
MESH = pl.DeviceIdType.MESH
LOG2E = math.log2(math.e)
VMEM_LIMIT = 60 * 1024 * 1024

TOK = 192
HEAD = 128
MEMBERS = 6
QW = MEMBERS * HEAD
SCORE_SCALE = LOG2E / math.sqrt(HEAD)
BIAS_SCALE = LOG2E / DISTANCE_SCALE

KV_PARTS = 4
KV_ROWS = TOK // KV_PARTS


def flip(value, low, high):
    value = value + low * (1 - 2 * (value % 2))
    return value + high * (3 - 2 * value)


def seq_peer(seq, moves):
    y, x, z = seq // 8, (seq // 2) % 4, seq % 2
    y = flip(y, moves[2], moves[3])
    x = flip(x, moves[0], moves[1])
    z = z + moves[4] * (1 - 2 * z)
    return (y * 4 + x) * 2 + z


def one_move(seq, direction):
    return seq_peer(seq, [1 if d == direction else 0 for d in range(5)])


def pick(value):
    return [value, value + 1 - 2 * (value % 2), (value + 2) % 4, 3 - value]


def place_moves(part, place):
    return [(place // 2 ** ((d - part) % 4)) % 2 for d in range(4)]


def enter(peers):
    barrier = pltpu.get_barrier_semaphore()
    for peer in peers:
        pl.semaphore_signal(barrier, inc=1, device_id=peer, device_id_type=MESH)
    pl.semaphore_wait(barrier, len(peers))


def send(src, dst, send_sem, recv_sem, peer):
    return pltpu.make_async_remote_copy(
        src_ref=src,
        dst_ref=dst,
        send_sem=send_sem,
        recv_sem=recv_sem,
        device_id=peer,
        device_id_type=MESH,
    )


NT = (((1,), (1,)), ((), ()))
TN = (((0,), (0,)), ((), ()))


def dot_nt(a, b):
    return lax.dot_general(a, b, NT, preferred_element_type=jnp.float32)


def dot_tn(a, b):
    return lax.dot_general(a, b, TN, preferred_element_type=jnp.float32)


def dot_nn(a, b):
    return jnp.dot(a, b, preferred_element_type=jnp.float32)


EDGE = 16
CH = 48


def gelu_value(inputs):
    return (
        0.5 * inputs * (1.0 + jnp.tanh(ROOT_TWO_PI * (inputs + CUBIC * inputs * inputs * inputs)))
    )


def gelu_slope(inputs):
    inner = jnp.tanh(ROOT_TWO_PI * (inputs + CUBIC * inputs * inputs * inputs))
    return 0.5 * (1.0 + inner) + 0.5 * inputs * (1.0 - inner * inner) * ROOT_TWO_PI * (
        1.0 + 3.0 * CUBIC * inputs * inputs
    )


def inverse_rms(values):
    return lax.rsqrt(jnp.mean(values * values, axis=-1, keepdims=True) + EPSILON)


def unpack_bases(words):
    lane = lax.broadcasted_iota(jnp.int32, (TOK, HEAD), 1)
    shift, letter = 2 * ((lane // 4) % 16), lane % 4
    blocks = []
    for j in range(4):
        word = jnp.where(lane < 64, words[:, 2 * j : 2 * j + 1], words[:, 2 * j + 1 : 2 * j + 2])
        field = jnp.bitwise_and(jnp.right_shift(word, shift), 3)
        blocks.append((field == letter).astype(jnp.float32))
    return jnp.concatenate(blocks, axis=1)


def halo(edge_ref, sems, seq):
    after = {"seq": (seq + 1) % 32}
    before = {"seq": (seq + 31) % 32}
    (send_a, recv_a), (send_b, recv_b) = sems
    return [
        send(edge_ref.at[pl.ds(TOK, EDGE)], edge_ref.at[pl.ds(0, EDGE)], send_a, recv_a, after),
        send(
            edge_ref.at[pl.ds(EDGE, EDGE)],
            edge_ref.at[pl.ds(EDGE + TOK, EDGE)],
            send_b,
            recv_b,
            before,
        ),
    ]


def with_edges(edge_ref, seq):
    blank = jnp.zeros((EDGE, QW), jnp.bfloat16)
    head_rows = jnp.where(seq > 0, edge_ref[0:EDGE], blank)
    tail_rows = jnp.where(seq < 31, edge_ref[EDGE + TOK :], blank)
    return jnp.concatenate([head_rows, edge_ref[EDGE : EDGE + TOK], tail_rows], axis=0)


HALF, THIRD = QW // 2, QW // 3
OUT_TURNS = (2, 0, 4)
WIDTHS = (THIRD, THIRD, THIRD, 2 * HEAD, HALF, HALF, HALF, HALF, HALF, HEAD, THIRD, THIRD, THIRD)
TURNS = (1, 2, 3, 4, 0, 1, 2, 3, 4, 4) + OUT_TURNS
PLACES = (32, 32, 32, 32, 16, 16, 16, 16, 16, 32, 4, 4, 4)
PARTS = len(WIDTHS)
EARLY = (0, 1, 2, 3)
LATE = (4, 5, 6, 7, 8)
EMBED = 9
OUTS = (10, 11, 12)
TAP_PAIRS = ((0, 1), (2, 3), (4, 4))


def chunk_owners(seq, turn, half):
    found = []
    for place in range(16 * half, 16 * half + 16):
        bits = [(place >> ((d - turn) % 5)) & 1 for d in range(5)]
        found.append(seq_peer(seq, bits))
    return found


def windows_of(padded, pair):
    turned = []
    for tap in sorted(set(pair)):
        window = padded[EDGE - 2 + tap : EDGE - 2 + tap + TOK].astype(jnp.float32).T
        turned.append(window.reshape(32, CH // 2, TOK))
    return jnp.concatenate([turned[0], turned[-1]], axis=1).astype(jnp.bfloat16)


def forward_kernel(
    slope_ref, shift_ref, words_ref, emb_w_ref, cot_ref, cw_hbm, qw_hbm, kvw_hbm, ow_hbm,
    att_ref, stat_ref, held_ref, q_ref, back_ref, hidden_ref, embedded_ref, normed_t_ref, cot_t_ref,
    win_ref, pwin_ref, edge_ref, act_land, turned_ref,
    cw_ref, qw_ref, kvw_ref, ow_ref, cot_full, kv_ref, normed_ref, acc_ref, top_ref, kpos_ref,
    load_sem, send_sem, recv_sem, hsend_sem, hrecv_sem, zsend_sem, zrecv_sem, msend_sem, mrecv_sem,
    asend_sem, arecv_sem,
):
    seq, tp = lax.axis_index("seq"), lax.axis_index("tp")
    loads = []
    for i, (far, near) in enumerate(
        ((ow_hbm, ow_ref), (cw_hbm, cw_ref), (qw_hbm, qw_ref), (kvw_hbm, kvw_ref))
    ):
        loads.append(pltpu.make_async_copy(far, near, load_sem.at[i]))
        loads[i].start()
    peers = [{"seq": one_move(seq, d)} for d in range(5)]
    side = {"tp": 1 - tp}
    enter(peers + [side, {"seq": (seq + 1) % 32}, {"seq": (seq + 31) % 32}])
    mine = pl.ds(pl.multiple_of(tp * QW, HEAD), QW)
    cot_copy = send(cot_ref, cot_full.at[:, mine], msend_sem.at[0], mrecv_sem.at[0], side)
    cot_copy.start()
    patches = unpack_bases(words_ref[...]).astype(jnp.bfloat16)
    embedded = dot_nn(patches, emb_w_ref[...]).astype(jnp.bfloat16)
    embedded_ref[...] = embedded
    embedded_wide = embedded.astype(jnp.float32)
    activated = gelu_value(embedded_wide * inverse_rms(embedded_wide))
    edge_ref[EDGE : EDGE + TOK] = activated.astype(jnp.bfloat16)
    edges = halo(
        edge_ref,
        ((msend_sem.at[1], mrecv_sem.at[1]), (msend_sem.at[2], mrecv_sem.at[2])),
        seq,
    )
    for copy in edges:
        copy.start()
    cot_full[:, mine] = cot_ref[...]
    cot_copy.wait()
    loads[0].wait()
    back_ref[...] = dot_nt(cot_full[...], ow_ref[...]).astype(jnp.bfloat16)
    for copy in edges:
        copy.wait()
    loads[1].wait()
    padded = with_edges(edge_ref, seq)
    edge_ref[...] = padded
    acts = []
    for d in range(5):
        copy = send(edge_ref, act_land.at[d], asend_sem.at[d], arecv_sem.at[d], peers[d])
        copy.start()
        acts.append(copy)
    hidden = embedded_ref[...].astype(jnp.float32)
    for tap in range(5):
        moved = dot_nn(padded, cw_ref[tap])
        hidden = hidden + moved[EDGE - 2 + tap : EDGE - 2 + tap + TOK]
    hidden_ref[:, mine] = hidden.astype(jnp.bfloat16)
    hidden_copy = send(
        hidden_ref.at[:, mine], hidden_ref.at[:, mine], msend_sem.at[3], mrecv_sem.at[3], side
    )
    hidden_copy.start()
    acc_ref[...] = jnp.zeros_like(acc_ref)
    top_ref[...] = jnp.full_like(top_ref, -1e30)
    hidden_copy.wait()
    loads[2].wait()
    loads[3].wait()
    hidden_wide = hidden_ref[...].astype(jnp.float32)
    normed_ref[...] = (hidden_wide * inverse_rms(hidden_wide)).astype(jnp.bfloat16)
    kv_ref[...] = dot_nn(normed_ref[...], kvw_ref[...]).astype(jnp.bfloat16)
    def own_half(half):
        rows = pl.ds(half * KV_ROWS, KV_ROWS)
        copies = []
        for k in (3, 2, 1, 0):
            for part in range(KV_PARTS):
                copy = send(
                    held_ref.at[0, part, rows],
                    held_ref.at[2**k, part, rows],
                    hsend_sem.at[half, k, part],
                    hrecv_sem.at[half, k, part],
                    peers[(part + k) % 4],
                )
                copy.start()
                copies.append((2**k, copy))
        return copies

    arrivals = {place: [] for place in range(1, 16)}

    def pass_on(place):
        for k in range(place.bit_length(), 4):
            for part in range(KV_PARTS):
                copy = send(
                    held_ref.at[place, part],
                    held_ref.at[2**k + place, part],
                    send_sem.at[2**k + place, part],
                    recv_sem.at[2**k + place, part],
                    peers[(part + k) % 4],
                )
                copy.start()
                arrivals[2**k + place].append(copy)

    def receive(*places_now):
        for place in places_now:
            for copy in arrivals[place]:
                copy.wait()
            pass_on(place)

    zcopies = []
    for part in range(KV_PARTS):
        rows = pl.ds(part * KV_ROWS, KV_ROWS)
        copy = send(
            kv_ref.at[rows],
            held_ref.at[0, part, pl.ds(KV_ROWS, KV_ROWS)],
            zsend_sem.at[part],
            zrecv_sem.at[part],
            peers[4],
        )
        copy.start()
        zcopies.append(copy)
    for part in range(KV_PARTS):
        held_ref[0, part, 0:KV_ROWS] = kv_ref[part * KV_ROWS : (part + 1) * KV_ROWS]
    first_half = own_half(0)
    q_ref[...] = dot_nn(normed_ref[...], qw_ref[...]).astype(jnp.bfloat16)
    column = lax.broadcasted_iota(jnp.int32, (TOK, 1), 0)
    qpos = (column + (seq * TOK + shift_ref[0])).astype(jnp.float32)
    lane = lax.broadcasted_iota(jnp.int32, (1, 2 * TOK), 1)
    ys, xs, zs = pick(seq // 8), pick((seq // 2) % 4), [seq % 2, 1 - seq % 2]
    for place in range(16):
        kpos = lane % KV_ROWS
        for part in range(KV_PARTS):
            m = place_moves(part, place)
            for z in range(2):
                source = (ys[m[2] ^ 3 * m[3]] * 4 + xs[m[0] ^ 3 * m[1]]) * 2 + zs[z]
                here = lane // KV_ROWS == 2 * part + z
                kpos = kpos + jnp.where(here, source * TOK + part * KV_ROWS, 0)
        kpos_ref[place] = kpos.astype(jnp.float32)

    def absorb(pair, kpos):
        keys = pair[:, :HEAD]
        values = jnp.concatenate([pair[:, HEAD:], jnp.ones_like(keys)], axis=1)
        distance = jnp.abs(qpos - kpos)
        for head in range(MEMBERS):
            scores = dot_nt(q_ref[:, head * HEAD : (head + 1) * HEAD], keys) * SCORE_SCALE
            scores = scores - distance * (slope_ref[head] * BIAS_SCALE)
            old = top_ref[head]
            new = jnp.maximum(old, jnp.max(scores, axis=1, keepdims=True))
            fading = jnp.exp2(old - new)
            weights = jnp.exp2(scores - new[:, :1]).astype(jnp.bfloat16)
            acc_ref[head] = acc_ref[head] * jnp.concatenate([fading, fading], axis=1) + dot_nn(
                weights, values
            )
            top_ref[head] = new

    def places(first, count):
        pair = held_ref[pl.ds(first, count)].reshape(count * 2 * TOK, 2 * HEAD)
        if count == 1:
            kpos = kpos_ref[first]
        else:
            kpos = jnp.concatenate([kpos_ref[first + i] for i in range(count)], axis=1)
        absorb(pair, kpos)

    def turned(ref, target, first, count):
        columns = slice(first * 2 * CH * 4, (first + count) * 2 * CH * 4)
        block = ref[:, columns].astype(jnp.float32).T.astype(jnp.bfloat16)
        target[8 * first : 8 * (first + count)] = block.reshape(8 * count, CH, TOK)

    def own_windows(i):
        win_ref[i] = windows_of(edge_ref, TAP_PAIRS[i])

    def peer_windows(i):
        turn = TURNS[LATE[i]]
        turned_ref[...] = windows_of(act_land.at[(turn + 4) % 5], TAP_PAIRS[i // 2])
        for j, owner in enumerate(chunk_owners(seq, turn, 0)):
            pwin_ref[i, j] = turned_ref[owner]

    for copy in zcopies:
        copy.wait()
    for place, copy in first_half + own_half(1):
        arrivals[place].append(copy)
    places(0, 1)
    own_windows(0)
    receive(1, 2, 4)
    own_windows(1)
    places(1, 2)
    receive(3, 5, 6)
    own_windows(2)
    places(3, 2)
    for copy in acts:
        copy.wait()
    receive(7)
    peer_windows(0)
    peer_windows(1)
    places(5, 3)
    peer_windows(2)
    peer_windows(3)
    peer_windows(4)
    receive(8, 9, 10, 11)
    places(8, 4)
    turned(cot_full, cot_t_ref, 0, 4)
    turned(normed_ref, normed_t_ref, 0, 4)
    receive(12, 13)
    places(12, 2)
    receive(14, 15)
    places(14, 2)
    lane = lax.broadcasted_iota(jnp.int32, (TOK, HEAD), 1)
    stats = jnp.zeros((TOK, HEAD), jnp.float32)
    for head in range(MEMBERS):
        totals = acc_ref[head, :, HEAD:]
        mixed = (acc_ref[head, :, :HEAD] / totals).astype(jnp.bfloat16)
        att_ref[:, head * HEAD : (head + 1) * HEAD] = mixed
        back = back_ref[:, head * HEAD : (head + 1) * HEAD].astype(jnp.float32)
        delta = jnp.sum(back * mixed.astype(jnp.float32), axis=1, keepdims=True)
        stats = jnp.where(lane == head, top_ref[head] + jnp.log2(totals), stats)
        stats = jnp.where(lane == 8 + head, delta, stats)
    turned_stats = stats.T
    for duo in range(MEMBERS // 2):
        for i in range(2):
            row = 2 * duo + i
            stat_ref[duo, :, i * TOK : (i + 1) * TOK] = turned_stats[row : row + 1]
            row = 2 * duo + i + 8
            stat_ref[3 + duo, :, i * TOK : (i + 1) * TOK] = turned_stats[row : row + 1]


def forward_attention(*operands):
    vmem = pl.BlockSpec(memory_space=pltpu.VMEM)
    f32, bf16 = jnp.float32, jnp.bfloat16
    return pl.pallas_call(
        forward_kernel,
        out_shape=(
            jax.ShapeDtypeStruct((TOK, QW), bf16),
            jax.ShapeDtypeStruct((6, 1, 2 * TOK), f32),
            jax.ShapeDtypeStruct((16, KV_PARTS, 2 * KV_ROWS, 2 * HEAD), bf16),
            jax.ShapeDtypeStruct((TOK, QW), bf16),
            jax.ShapeDtypeStruct((TOK, QW), bf16),
            jax.ShapeDtypeStruct((TOK, 2 * QW), bf16),
            jax.ShapeDtypeStruct((TOK, QW), bf16),
            jax.ShapeDtypeStruct((32, CH, TOK), bf16),
            jax.ShapeDtypeStruct((32, CH, TOK), bf16),
            jax.ShapeDtypeStruct((3, 32, CH, TOK), bf16),
            jax.ShapeDtypeStruct((5, 16, CH, TOK), bf16),
        ),
        in_specs=[pl.BlockSpec(memory_space=pltpu.SMEM)] * 2
        + [vmem] * 3
        + [pl.BlockSpec(memory_space=pl.ANY)] * 4,
        out_specs=(vmem,) * 11,
        scratch_shapes=[
            pltpu.VMEM((TOK + 2 * EDGE, QW), bf16),
            pltpu.VMEM((5, TOK + 2 * EDGE, QW), bf16),
            pltpu.VMEM((32, CH, TOK), bf16),
            pltpu.VMEM((5, QW, QW), bf16),
            pltpu.VMEM((2 * QW, QW), bf16),
            pltpu.VMEM((2 * QW, 2 * HEAD), bf16),
            pltpu.VMEM((QW, 2 * QW), bf16),
            pltpu.VMEM((TOK, 2 * QW), bf16),
            pltpu.VMEM((TOK, 2 * HEAD), bf16),
            pltpu.VMEM((TOK, 2 * QW), bf16),
            pltpu.VMEM((MEMBERS, TOK, 2 * HEAD), f32),
            pltpu.VMEM((MEMBERS, TOK, HEAD), f32),
            pltpu.VMEM((16, 1, 2 * TOK), f32),
            pltpu.SemaphoreType.DMA((4,)),
            pltpu.SemaphoreType.DMA((16, KV_PARTS)),
            pltpu.SemaphoreType.DMA((16, KV_PARTS)),
            pltpu.SemaphoreType.DMA((2, 4, KV_PARTS)),
            pltpu.SemaphoreType.DMA((2, 4, KV_PARTS)),
            pltpu.SemaphoreType.DMA((KV_PARTS,)),
            pltpu.SemaphoreType.DMA((KV_PARTS,)),
            pltpu.SemaphoreType.DMA((4,)),
            pltpu.SemaphoreType.DMA((4,)),
            pltpu.SemaphoreType.DMA((5,)),
            pltpu.SemaphoreType.DMA((5,)),
        ],
        compiler_params=pltpu.CompilerParams(
            collective_id=0, has_side_effects=True, vmem_limit_bytes=VMEM_LIMIT
        ),
    )(*operands)


class Halving:
    def __init__(self, turns, sums, lands, send_sem, recv_sem, seq):
        self.turns, self.sums, self.lands = turns, sums, lands
        self.send_sem, self.recv_sem = send_sem, recv_sem
        self.peers = [{"seq": one_move(seq, d)} for d in range(5)]
        self.seq, self.flights = seq, {}

    def owners(self, part, half):
        return chunk_owners(self.seq, self.turns[part], half)

    def start(self, part, k):
        copies = []
        if k > 0:
            spans = ((2 ** (k - 1), 2 ** (k - 1)), (0, 2 ** (k - 1)))
        else:
            spans = ((0, 1),)
        for piece, (low, count) in enumerate(spans):
            copy = send(
                self.sums[part].at[pl.ds(2**k + low, count)],
                self.lands[part].at[pl.ds(2**k + low, count)],
                self.send_sem.at[part, k, piece],
                self.recv_sem.at[part, k, piece],
                self.peers[(self.turns[part] + k) % 5],
            )
            copy.start()
            copies.append((copy, low, count))
        return copies

    def settle(self, part, k, item):
        copy, low, count = item
        copy.wait()
        bunch = min(count, 4)
        total, landed = self.sums[part], self.lands[part]

        def add(i, carry):
            at = pl.ds(low + i * bunch, bunch)
            total[at] = total[at] + landed[pl.ds(2**k + low + i * bunch, bunch)]
            return carry

        lax.fori_loop(0, count // bunch, add, 0)

    def launch(self, part, k=4):
        self.flights[part] = self.start(part, k)

    def advance(self, parts, k):
        following = {}
        for part in parts:
            self.settle(part, k, self.flights[part][0])
            following[part] = self.start(part, k - 1)
        for part in parts:
            self.settle(part, k, self.flights[part][1])
        self.flights.update(following)


def chunk_rows(ref, owners, count):
    return jnp.concatenate([ref[owner, 0:count] for owner in owners], axis=0)


OUT_PARTS = len(OUTS)
OUT_WIDTH = THIRD


def backward_kernel(
    slope_ref, shift_ref, q_ref, back_ref, held_ref, stat_ref, cot_t_ref, att_ref,
    dq_ref, dkv_ref, out_ref,
    qs_ref, bs_ref, dq_acc, part_ref, land3, land2, land1, land0, landz,
    sums0, sums1, sums2, lands0, lands1, lands2,
    send_sem, recv_sem, zsend_sem, zrecv_sem, osend_sem, orecv_sem,
):
    seq = lax.axis_index("seq")
    peers = [{"seq": one_move(seq, d)} for d in range(5)]
    enter(peers)
    outs = Halving(
        OUT_TURNS, (sums0, sums1, sums2), (lands0, lands1, lands2), osend_sem, orecv_sem, seq
    )
    out_parts = range(OUT_PARTS)

    def fill(part, half):
        columns = slice(part * OUT_WIDTH, (part + 1) * OUT_WIDTH)
        grads = dot_nn(chunk_rows(cot_t_ref, outs.owners(part, half), CH), att_ref[:, columns])
        outs.sums[part][16 * half : 16 * half + 16] = grads.astype(jnp.bfloat16).reshape(
            16, CH, OUT_WIDTH
        )

    for part in out_parts:
        fill(part, 1)
        outs.launch(part)
    lands = [land0, land1, land2, land3]
    for head in range(MEMBERS):
        rows = slice(head * TOK, (head + 1) * TOK)
        qs_ref[rows] = q_ref[:, head * HEAD : (head + 1) * HEAD]
        bs_ref[rows] = back_ref[:, head * HEAD : (head + 1) * HEAD]
    dq_acc[...] = jnp.zeros_like(dq_acc)
    lane = lax.broadcasted_iota(jnp.int32, (1, 2 * TOK), 1)
    qpos = (lane % TOK + (seq * TOK + shift_ref[0])).astype(jnp.float32)
    slopes = [
        jnp.where(lane < TOK, slope_ref[2 * duo], slope_ref[2 * duo + 1]) * BIAS_SCALE
        for duo in range(MEMBERS // 2)
    ]
    row = lax.broadcasted_iota(jnp.int32, (KV_ROWS, 1), 0)

    def work(first, count):
        size = count * 2 * TOK
        pair = held_ref[pl.ds(first, count)].reshape(size, 2 * HEAD)
        keys, values = pair[:, :HEAD], pair[:, HEAD:]
        kpos = []
        for i in range(count):
            for part in range(KV_PARTS):
                for z in range(2):
                    source = seq_peer(seq, place_moves(part, first + i) + [z])
                    kpos.append(row + (source * TOK + part * KV_ROWS))
        distance = jnp.abs(qpos - jnp.concatenate(kpos, axis=0).astype(jnp.float32))
        all_probs, all_grads = [], []
        for duo in range(MEMBERS // 2):
            rows = slice(duo * 2 * TOK, (duo + 1) * 2 * TOK)
            scores = dot_nt(keys, qs_ref[rows]) * SCORE_SCALE - distance * slopes[duo]
            probs = jnp.exp2(scores - stat_ref[duo])
            back_probs = dot_nt(values, bs_ref[rows])
            all_grads.append((probs * (back_probs - stat_ref[3 + duo])).astype(jnp.bfloat16))
            all_probs.append(probs.astype(jnp.bfloat16))
        grad_scores = jnp.concatenate(all_grads, axis=1)
        value_grad = dot_nn(jnp.concatenate(all_probs, axis=1), bs_ref[...])
        key_grad = dot_nn(grad_scores, qs_ref[...])
        dq_acc[...] += dot_tn(grad_scores, keys)
        both = jnp.concatenate([key_grad * (1.0 / math.sqrt(HEAD)), value_grad], axis=1)
        part_ref[pl.ds(first, count)] = both.astype(jnp.bfloat16).reshape(
            count, KV_PARTS, 2 * KV_ROWS, 2 * HEAD
        )

    def piece_copies(number, k, first, count):
        return [
            send(
                part_ref.at[pl.ds(first, count), part],
                lands[k].at[pl.ds(first - 2**k, count), part],
                send_sem.at[number, part],
                recv_sem.at[number, part],
                peers[(part + k) % 4],
            )
            for part in range(KV_PARTS)
        ]

    def start_piece(*piece):
        copies = piece_copies(*piece)
        for copy in copies:
            copy.start()
        return copies

    def take_in(place, stages, pieces):
        for copies in pieces:
            for copy in copies:
                copy.wait()
        total = part_ref[place].astype(jnp.float32)
        for k in stages:
            total = total + lands[k][place].astype(jnp.float32)
        part_ref[place] = total.astype(jnp.bfloat16)

    def outer_places(i, carry):
        first = 14 - 2 * i
        work(first, 2)
        for copy in piece_copies(i, 3, first, 2):
            copy.start()
        return carry

    def inner_places(i, carry):
        work(2 * i, 2)
        return carry

    for part in out_parts:
        fill(part, 0)
    lax.fori_loop(0, 4, outer_places, 0)
    third = [piece_copies(i, 3, 14 - 2 * i, 2) for i in range(4)]
    outs.advance(out_parts, 4)
    lax.fori_loop(3, 4, inner_places, 0)
    take_in(6, (3,), [third[0]])
    take_in(7, (3,), [])
    second = [start_piece(4, 2, 6, 2)]
    lax.fori_loop(2, 3, inner_places, 0)
    take_in(4, (3,), [third[1]])
    take_in(5, (3,), [])
    second.append(start_piece(5, 2, 4, 2))
    outs.advance(out_parts, 3)
    lax.fori_loop(1, 2, inner_places, 0)
    take_in(2, (2, 3), [third[2], second[0]])
    take_in(3, (2, 3), [])
    first = start_piece(6, 1, 2, 2)
    lax.fori_loop(0, 1, inner_places, 0)
    take_in(1, (1, 2, 3), [third[3], second[1], first])
    last = start_piece(7, 0, 1, 1)
    for part in out_parts:
        for item in outs.flights[part]:
            outs.settle(part, 2, item)
        out_ref[part] = outs.sums[part][0:4]
    take_in(0, (0, 1, 2, 3), [last])
    zcopies = []
    for part in range(KV_PARTS):
        copy = send(
            part_ref.at[0, part, pl.ds(KV_ROWS, KV_ROWS)],
            landz.at[part],
            zsend_sem.at[part],
            zrecv_sem.at[part],
            peers[4],
        )
        copy.start()
        zcopies.append(copy)
    for head in range(MEMBERS):
        grad = dq_acc[head * TOK : (head + 1) * TOK] * (1.0 / math.sqrt(HEAD))
        dq_ref[:, head * HEAD : (head + 1) * HEAD] = grad.astype(jnp.bfloat16)
    for part in range(KV_PARTS):
        zcopies[part].wait()
        dkv_ref[part * KV_ROWS : (part + 1) * KV_ROWS] = part_ref[0, part, 0:KV_ROWS] + landz[part]


def backward_attention(*operands):
    vmem = pl.BlockSpec(memory_space=pltpu.VMEM)
    f32, bf16 = jnp.float32, jnp.bfloat16
    block = (KV_PARTS, 2 * KV_ROWS, 2 * HEAD)
    return pl.pallas_call(
        backward_kernel,
        out_shape=(
            jax.ShapeDtypeStruct((TOK, QW), bf16),
            jax.ShapeDtypeStruct((TOK, 2 * HEAD), bf16),
            jax.ShapeDtypeStruct((OUT_PARTS, 4, CH, OUT_WIDTH), bf16),
        ),
        in_specs=[pl.BlockSpec(memory_space=pltpu.SMEM)] * 2 + [vmem] * 6,
        out_specs=(vmem,) * 3,
        scratch_shapes=[
            pltpu.VMEM((MEMBERS * TOK, HEAD), bf16),
            pltpu.VMEM((MEMBERS * TOK, HEAD), bf16),
            pltpu.VMEM((MEMBERS * TOK, HEAD), f32),
            pltpu.VMEM((16,) + block, bf16),
            pltpu.VMEM((8,) + block, bf16),
            pltpu.VMEM((4,) + block, bf16),
            pltpu.VMEM((2,) + block, bf16),
            pltpu.VMEM((1,) + block, bf16),
            pltpu.VMEM((KV_PARTS, KV_ROWS, 2 * HEAD), bf16),
        ]
        + [pltpu.VMEM((32, CH, OUT_WIDTH), bf16)] * 6
        + [
            pltpu.SemaphoreType.DMA((8, KV_PARTS)),
            pltpu.SemaphoreType.DMA((8, KV_PARTS)),
            pltpu.SemaphoreType.DMA((KV_PARTS,)),
            pltpu.SemaphoreType.DMA((KV_PARTS,)),
            pltpu.SemaphoreType.DMA((OUT_PARTS, 5, 2)),
            pltpu.SemaphoreType.DMA((OUT_PARTS, 5, 2)),
        ],
        compiler_params=pltpu.CompilerParams(
            collective_id=1, has_side_effects=True, vmem_limit_bytes=VMEM_LIMIT
        ),
    )(*operands)


def weights_kernel(
    normed_ref, words_ref, outs_ref,
    dq_ref, att_ref, pair_ref, hidden_ref, embedded_ref, cotangent_ref,
    win_hbm, pwin_hbm, cw_hbm, qw_hbm, kvw_hbm, ow_hbm,
    result_out, query_out, output_out, pair_out, conv_out, embed_out,
    *scratch, factor,
):
    sums, lands = scratch[:PARTS], scratch[PARTS : 2 * PARTS]
    dp_lands = scratch[2 * PARTS : 3 * PARTS]
    (
        cw_ref, qw_ref, kvw_ref, ow_ref, win_ref, pwin_ref, conv_land, patch_ref, out_own, out_side,
        wide_own, wide_side, edge_ref, conv_side, active_own, active_side, emb_ref,
        land_tp, land_diag, load_sem, send_sem, recv_sem, fsend_sem, frecv_sem, csend_sem, crecv_sem,
    ) = scratch[3 * PARTS :]
    seq, dp, tp = lax.axis_index("seq"), lax.axis_index("dp"), lax.axis_index("tp")
    loads = []
    for i, (far, near) in enumerate(
        (
            (qw_hbm, qw_ref), (kvw_hbm, kvw_ref), (cw_hbm, cw_ref), (win_hbm, win_ref),
            (pwin_hbm, pwin_ref), (ow_hbm, ow_ref),
        )
    ):
        loads.append(pltpu.make_async_copy(far, near, load_sem.at[i]))
        loads[i].start()
    peers = [{"seq": one_move(seq, d)} for d in range(5)]
    over = {"dp": 1 - dp}
    side = {"tp": 1 - tp}
    diagonal = {"dp": 1 - dp, "tp": 1 - tp}
    around = [{"seq": (seq + 1) % 32}, {"seq": (seq + 31) % 32}]
    enter(peers + [over, side, diagonal] + around)
    left_rows = lax.broadcasted_iota(jnp.int32, (16 * CH, HALF), 0) % CH < CH // 2

    run = Halving(TURNS, sums, lands, send_sem, recv_sem, seq)
    conv = slice(EDGE, EDGE + TOK)

    def fill(part, half):
        owners = run.owners(part, half)
        if part < 3:
            columns = slice(part * THIRD, (part + 1) * THIRD)
            grads = dot_nn(chunk_rows(normed_ref, owners, CH), dq_ref[:, columns])
        elif part == 3:
            grads = dot_nn(chunk_rows(normed_ref, owners, CH), pair_ref[...])
        else:
            columns = pl.ds(pl.multiple_of(tp * HALF, HEAD), HALF)
            emb = dot_nn(chunk_rows(patch_ref, owners, 16), emb_ref[:, columns])
            grads = jnp.concatenate(
                [
                    emb[16 * j : 16 * j + 16, HEAD * c : HEAD * c + HEAD]
                    for j in range(16)
                    for c in range(3)
                ],
                axis=0,
            )
        sums[part][16 * half : 16 * half + 16] = grads.astype(jnp.bfloat16).reshape(
            16, CH, WIDTHS[part]
        )

    def conv_columns(part):
        if part == LATE[4]:
            return slice(0, QW)
        return slice((part - LATE[0]) % 2 * HALF, ((part - LATE[0]) % 2 + 1) * HALF)

    def conv_exchange(part):
        i, columns = part - LATE[0], conv_columns(part)
        width = columns.stop - columns.start
        copy = send(
            edge_ref.at[pl.ds(EDGE, TOK), pl.ds(columns.start, width)],
            conv_land.at[i, :, pl.ds(0, width)],
            csend_sem.at[i],
            crecv_sem.at[i],
            run.peers[(TURNS[part] + 4) % 5],
        )
        copy.start()
        return copy

    def fill_conv(part):
        i, columns = part - LATE[0], conv_columns(part)
        width = columns.stop - columns.start
        own_rows = chunk_rows(win_ref.at[i // 2], run.owners(part, 0), CH)
        peer_rows = pwin_ref[i].reshape(16 * CH, TOK)
        grads = dot_nn(own_rows, edge_ref[conv, columns]) + dot_nn(
            peer_rows, conv_land[i, :, :width]
        )
        if part == LATE[4]:
            grads = jnp.where(left_rows, grads[:, :HALF], grads[:, HALF:])
        sums[part][...] = grads.astype(jnp.bfloat16).reshape(16, CH, HALF)

    finals = {}

    def finish(parts):
        for part in parts:
            run.settle(part, 0, run.flights[part][0])
            copy = send(
                sums[part].at[0], dp_lands[part], fsend_sem.at[part], frecv_sem.at[part], over
            )
            copy.start()
            finals[part] = copy

    def total(part):
        finals[part].wait()
        return (sums[part][0].astype(jnp.float32) + dp_lands[part][...].astype(jnp.float32)) * factor

    for part in EARLY:
        fill(part, 1)
        run.launch(part)
    for i, part in enumerate(OUTS):
        sums[part][...] = outs_ref[i]
        run.launch(part, 1)
    loads[0].wait()
    loads[1].wait()
    partial = dot_nt(dq_ref[...], qw_ref[...]) + dot_nt(pair_ref[...], kvw_ref[...])
    wide_own[...] = partial.astype(jnp.bfloat16)
    wide_copy = send(wide_own, wide_side, fsend_sem.at[PARTS + 0], frecv_sem.at[PARTS + 0], side)
    wide_copy.start()
    for part in EARLY:
        fill(part, 0)
    patches = unpack_bases(words_ref[...]).T
    patch_ref[...] = patches.reshape(32, 16, TOK).astype(jnp.bfloat16)
    hidden = hidden_ref[...].astype(jnp.float32)
    scale = inverse_rms(hidden)
    wide_copy.wait()
    back_normed = wide_own[...].astype(jnp.float32) + wide_side[...].astype(jnp.float32)
    mean = jnp.mean(back_normed * (hidden * scale), axis=-1, keepdims=True)
    mine = pl.ds(pl.multiple_of(tp * QW, HEAD), QW)
    own = wide_own[:, mine].astype(jnp.float32) + wide_side[:, mine].astype(jnp.float32)
    normed = hidden_ref[:, mine].astype(jnp.float32) * scale
    back_hidden = cotangent_ref[...].astype(jnp.float32) + scale * (own - normed * mean)
    edge_ref[EDGE : EDGE + TOK] = back_hidden.astype(jnp.bfloat16)
    edge_copies = halo(
        edge_ref,
        ((fsend_sem.at[PARTS + 1], frecv_sem.at[PARTS + 1]), (fsend_sem.at[PARTS + 2], frecv_sem.at[PARTS + 2])),
        seq,
    )
    for copy in edge_copies:
        copy.start()
    conv_copy = send(
        edge_ref.at[pl.ds(EDGE, TOK)], conv_side, fsend_sem.at[PARTS + 3], frecv_sem.at[PARTS + 3], side
    )
    conv_copy.start()
    exchanges = {part: conv_exchange(part) for part in LATE}
    for i in range(2, 5):
        loads[i].wait()
    for copy in edge_copies:
        copy.wait()
    padded = with_edges(edge_ref, seq)
    active = jnp.zeros((TOK, QW), jnp.float32)
    for tap in range(5):
        moved = dot_nt(padded, cw_ref[tap])
        active = active + moved[EDGE + 2 - tap : EDGE + 2 - tap + TOK]
    active_own[...] = active.astype(jnp.bfloat16)
    active_copy = send(active_own, active_side, fsend_sem.at[PARTS + 4], frecv_sem.at[PARTS + 4], side)
    active_copy.start()
    loads[5].wait()
    out_own[...] = dot_nn(att_ref[...], ow_ref[...]).astype(jnp.bfloat16)
    theirs = pl.ds(pl.multiple_of((1 - tp) * QW, HEAD), QW)
    out_copy = send(out_own.at[:, theirs], out_side, fsend_sem.at[PARTS + 7], frecv_sem.at[PARTS + 7], side)
    out_copy.start()
    run.advance(EARLY, 4)
    run.advance(OUTS, 1)
    for part in LATE:
        exchanges[part].wait()
        fill_conv(part)
        run.launch(part, 3)
    embedded = embedded_ref[...].astype(jnp.float32)
    scale_in = inverse_rms(embedded)
    normed_in = embedded * scale_in
    slope = gelu_slope(normed_in)
    conv_copy.wait()
    residual = edge_ref[EDGE : EDGE + TOK].astype(jnp.float32) + conv_side[...].astype(jnp.float32)
    active_copy.wait()
    back_in = (active_own[...].astype(jnp.float32) + active_side[...].astype(jnp.float32)) * slope
    mean_in = jnp.mean(back_in * normed_in, axis=-1, keepdims=True)
    emb_ref[...] = (residual + scale_in * (back_in - normed_in * mean_in)).astype(jnp.bfloat16)
    fill(EMBED, 1)
    run.launch(EMBED)
    fill(EMBED, 0)
    run.advance(EARLY, 3)
    finish(OUTS)
    out_copy.wait()
    projected = out_own[:, mine].astype(jnp.float32) + out_side[...].astype(jnp.float32)
    result_out[...] = (hidden_ref[:, mine].astype(jnp.float32) + projected).astype(jnp.bfloat16)
    run.advance((EMBED,), 4)
    run.advance(LATE, 3)
    run.advance(EARLY, 2)
    run.advance((EMBED,), 3)
    run.advance(LATE, 2)
    run.advance(EARLY, 1)
    run.advance((EMBED,), 2)
    finish(EARLY)
    run.advance(LATE, 1)
    run.advance((EMBED,), 1)
    finish(LATE + (EMBED,))
    sidecopy = send(sums[EMBED].at[0], land_tp, fsend_sem.at[PARTS + 5], frecv_sem.at[PARTS + 5], side)
    sidecopy.start()
    diagcopy = send(sums[EMBED].at[0], land_diag, fsend_sem.at[PARTS + 6], frecv_sem.at[PARTS + 6], diagonal)
    diagcopy.start()
    for third in range(3):
        query_out[:, third * THIRD : (third + 1) * THIRD] = total(third)
    pair_out[...] = total(3)
    for third in range(3):
        output_out[:, third * THIRD : (third + 1) * THIRD] = total(OUTS[third])
    rows = CH // 2
    for part in range(4):
        tap, columns = part // 2 * 2, slice(part % 2 * HALF, (part % 2 + 1) * HALF)
        block = total(LATE[part])
        conv_out[tap, :, columns] = block[:rows]
        conv_out[tap + 1, :, columns] = block[rows:]
    block = total(LATE[4])
    conv_out[4, :, :HALF] = block[:rows]
    conv_out[4, :, HALF:] = block[rows:]

    def embed_store(block, core):
        wide = jnp.concatenate([block[:16], block[16:32], block[32:]], axis=1)
        embed_out[:, pl.ds(pl.multiple_of(core * HALF, HEAD), HALF)] = wide

    embed_store(total(EMBED), tp)
    sidecopy.wait()
    diagcopy.wait()
    other = land_tp[...].astype(jnp.float32) + land_diag[...].astype(jnp.float32)
    embed_store(other * factor, 1 - tp)


def weight_gradients(factor, *operands):
    vmem = pl.BlockSpec(memory_space=pltpu.VMEM)
    f32, bf16 = jnp.float32, jnp.bfloat16
    return pl.pallas_call(
        functools.partial(weights_kernel, factor=factor),
        out_shape=(
            jax.ShapeDtypeStruct((TOK, QW), bf16),
            jax.ShapeDtypeStruct((CH, QW), f32),
            jax.ShapeDtypeStruct((CH, QW), f32),
            jax.ShapeDtypeStruct((CH, 2 * HEAD), f32),
            jax.ShapeDtypeStruct((5, CH // 2, QW), f32),
            jax.ShapeDtypeStruct((16, QW), f32),
        ),
        in_specs=[vmem] * 9 + [pl.BlockSpec(memory_space=pl.ANY)] * 6,
        out_specs=(vmem,) * 6,
        scratch_shapes=[pltpu.VMEM((n, CH, w), bf16) for n, w in zip(PLACES, WIDTHS)] * 2
        + [pltpu.VMEM((CH, w), bf16) for w in WIDTHS]
        + [
            pltpu.VMEM((5, QW, QW), bf16),
            pltpu.VMEM((2 * QW, QW), bf16),
            pltpu.VMEM((2 * QW, 2 * HEAD), bf16),
            pltpu.VMEM((QW, 2 * QW), bf16),
            pltpu.VMEM((3, 32, CH, TOK), bf16),
            pltpu.VMEM((5, 16, CH, TOK), bf16),
            pltpu.VMEM((5, TOK, QW), bf16),
            pltpu.VMEM((32, 16, TOK), bf16),
            pltpu.VMEM((TOK, 2 * QW), bf16),
            pltpu.VMEM((TOK, QW), bf16),
            pltpu.VMEM((TOK, 2 * QW), bf16),
            pltpu.VMEM((TOK, 2 * QW), bf16),
            pltpu.VMEM((TOK + 2 * EDGE, QW), bf16),
            pltpu.VMEM((TOK, QW), bf16),
            pltpu.VMEM((TOK, QW), bf16),
            pltpu.VMEM((TOK, QW), bf16),
            pltpu.VMEM((TOK, QW), bf16),
            pltpu.VMEM((CH, HEAD), bf16),
            pltpu.VMEM((CH, HEAD), bf16),
            pltpu.SemaphoreType.DMA((6,)),
            pltpu.SemaphoreType.DMA((PARTS, 5, 2)),
            pltpu.SemaphoreType.DMA((PARTS, 5, 2)),
            pltpu.SemaphoreType.DMA((PARTS + 8,)),
            pltpu.SemaphoreType.DMA((PARTS + 8,)),
            pltpu.SemaphoreType.DMA((5,)),
            pltpu.SemaphoreType.DMA((5,)),
        ],
        compiler_params=pltpu.CompilerParams(
            collective_id=2, has_side_effects=True, vmem_limit_bytes=VMEM_LIMIT
        ),
    )(*operands)


def last_kernel(*refs):
    result, query, output, pair, conv, embed = refs[:6]
    result_out, query_out, output_out, pair_out, conv_out, embed_out = refs[6:]
    result_out[...] = result[...]
    query_out[...] = query[...]
    output_out[...] = output[...]
    pair_out[:, 0, :] = pair[...]
    conv_out[...] = conv[...]
    embed_out[...] = embed[...]


def write_outputs(*operands):
    vmem = pl.BlockSpec(memory_space=pltpu.VMEM)
    shapes = [jax.ShapeDtypeStruct(o.shape, o.dtype) for o in operands]
    shapes[3] = jax.ShapeDtypeStruct((CH, 1, 2 * HEAD), jnp.float32)
    return pl.pallas_call(
        last_kernel,
        out_shape=tuple(shapes),
        in_specs=[vmem] * 6,
        out_specs=(vmem,) * 6,
    )(*operands)


def per_device(
    bases,
    shifts,
    embed_weight,
    conv_weight,
    query_weight,
    keyvalue_weight,
    output_weight,
    slopes,
    cotangent,
):
    tokens = cotangent.shape[1]
    words = bases.reshape(tokens, -1)
    pair_weight = keyvalue_weight.reshape(2 * QW, 2 * HEAD)
    cotangent_local = cotangent[0]
    factor = (lax.axis_size("dp") * lax.axis_size("seq") * tokens) ** (-0.5)
    (
        attended, stats, held, queries, back_attended, hidden, embedded, normed_t, cot_t, win, peer_win
    ) = forward_attention(
        slopes,
        shifts,
        words,
        embed_weight,
        cotangent_local,
        conv_weight,
        query_weight,
        pair_weight,
        output_weight,
    )
    back_query, back_pair, outs = backward_attention(
        slopes, shifts, queries, back_attended, held, stats, cot_t, attended
    )
    result, grad_query, grad_output, grad_pair, grad_conv, grad_embed = weight_gradients(
        factor,
        normed_t,
        words,
        outs,
        back_query,
        attended,
        back_pair,
        hidden,
        embedded,
        cotangent_local,
        win,
        peer_win,
        conv_weight,
        query_weight,
        pair_weight,
        output_weight,
    )
    result, grad_query, grad_output, grad_pair, grad_conv, grad_embed = write_outputs(
        result, grad_query, grad_output, grad_pair, grad_conv, grad_embed
    )
    return (result[None], grad_embed, grad_conv, grad_query, grad_pair, grad_output.T)


def solution(mesh):
    placed = (
        P("dp", "seq"),
        P("dp"),
        P(),
        P(None, None, "tp"),
        P(None, "tp"),
        P(None, "tp", None),
        P("tp", None),
        P("tp"),
        P("dp", "seq", "tp"),
    )
    return jax.shard_map(
        per_device,
        mesh=mesh,
        in_specs=placed,
        out_specs=(
            P("dp", "seq", "tp"),
            P("seq", None),
            P(None, "seq", "tp"),
            P("seq", "tp"),
            P("seq", "tp", None),
            P("tp", "seq"),
        ),
        check_vma=False,
    )
```
